128 devices in a mesh: scen: 8 (over y_lo, z), area: 16 (over y_hi, x, core).
Axes of the slice: x: 4, y: 4 (y_hi: 2, y_lo: 2; y = y_hi * 2 + y_lo), z: 4, core: 2. Of those that a mesh axis runs over, the one named last changes fastest.
Arguments:
- demand: bfloat16 [128, 48, 10000], P('scen', None, 'area'), may hold values from 0.5 to 1.5
- ptdf: bfloat16 [10000, 2000], P('area'), may hold values from -0.0625 to 0.0625
- branch_limits: float32 [12000], replicated, may hold values from 0.2 to 1.5
- line_ids: int32 [2000], replicated, may hold values from 0 to 11999, as said below
- unit_bus: int32 [4000], P('area'), may hold values from 0 to 624
- node_map: int32 [4, 128], replicated, may hold values from 0 to 63, as said below
- cost_linear: float32 [4000], P('area'), may hold values from -3 to 3
- cost_quad: float32 [4000], P('area'), may hold values from 0.5 to 2
- capacity: float32 [4000], P('area'), may hold values from 0.5 to 2
- ramp_limits: float32 [4000], P('area'), may hold values from 0.05 to 0.5
- gen_init: float32 [128, 48, 4000], P('scen', None, 'area'), may hold values from 0 to 1
- price_init: float32 [128, 48, 4000], P('scen', None, 'area'), may hold values from -2 to 2
Outputs:
- dispatch: float32 [128, 48, 4000], P('scen', None, 'area')
- prices: float32 [128, 48, 4000], P('scen', None, 'area')
The draws below stay inside these ranges and needn't reach their ends.
Inputs may be any that keep to these rules, and one draw needn't show every extreme that they name: `line_ids`: distinct branch indices. Section 1 has node 0 only; at section k node_map[k, s] = leaf(s) * w_k // 64 with w_k = 1, 4, 8, 64 and leaf(s) the last-section node; every last-section node holds exactly two scenarios. `unit_bus`: A unit's bus lies in the unit's own area.
All inputs are finite; a program needn't handle non-finite values.
Results may differ from the reference program's by a relative error of at most 0.0011.
Values may be sent and summed in bfloat16 or wider, within the bound.
No kernel may reach another device: no remote copies, remote signals or barrier semaphores. Data moves between devices by JAX's collectives and lax.ppermute only.
A program may use at most 128 MiB of HBM per device.

```python
import math
import jax
import jax.numpy as jnp
from jax import lax

BUSES = 10000
UNITS = 4000
LINES = 2000
BRANCHES = 12000
HOURS = 48
SECTION2_NODES = 4
SECTION3_NODES = 8
ITERS = 2
SCENARIOS = 128
N_AREA = 16


def draw_node_map(key, part):
    key = jax.random.fold_in(key, 7)
    leaves = SCENARIOS // 2
    order = jax.random.permutation(key, SCENARIOS).astype(jnp.int32)
    leaf = order % leaves
    widths = [1, SECTION2_NODES, SECTION3_NODES, leaves]
    return jnp.stack([leaf * width // leaves for width in widths]).astype(jnp.int32)


def draw_line_ids(key, part):
    key = jax.random.fold_in(key, 11)
    return jax.random.permutation(key, BRANCHES)[:LINES].astype(jnp.int32)


def plant(entries, stream_key, smallest, high):
    shape = entries.shape
    spot = [jax.random.randint(jax.random.fold_in(stream_key, axis), (), 0, shape[axis]) for axis in range(len(shape))]
    entries = entries.at[tuple(spot)].set(smallest)
    longest = shape.index(max(shape))
    spot[longest] = (spot[longest] + 1) % shape[longest]
    return entries.at[tuple(spot)].set(high)


def steps_of(rng, extent, split, least, largest):
    def one(dim, shards_of):
        heights = jax.random.uniform(jax.random.fold_in(jax.random.fold_in(rng, 6), dim), (shards_of,), jnp.float32, least / len(split), largest / len(split))
        return jnp.repeat(jnp.exp(heights), extent[dim] // shards_of).reshape((-1,) + (1,) * (len(extent) - dim - 1))

    factor_of = one(*split[0])
    for cut in split[1:]:
        factor_of = factor_of * one(*cut)
    return factor_of


def scatter_about(key, shape, scale, most, cuts=(), held_as=jnp.bfloat16):
    gain = steps_of(key, shape, cuts, -0.22, 0.18) if cuts else 1.0
    values = jax.random.normal(key, shape, jnp.float32) * scale * gain
    return jnp.minimum(jnp.maximum(values, -most), most).astype(held_as)


def setup_inputs(seed: int = 0) -> dict:
    key_list = jax.random.split(jax.random.key(seed), 13)
    demand = jnp.clip(0.5 + 1.0 * jax.random.uniform(key_list[0], (SCENARIOS, HOURS, BUSES), jnp.float32) ** steps_of(key_list[0], (SCENARIOS, HOURS, BUSES), ((0, 8), (2, 16)), -0.2, 0.2), 0.5, 1.5).astype(jnp.bfloat16)
    ptdf = scatter_about(key_list[1], (BUSES, LINES), BUSES ** -0.5, 0.0625, ((0, 16),))
    branch_limits = jnp.clip(jnp.exp(jax.random.uniform(key_list[2], (BRANCHES,), jnp.float32, math.log(0.2), math.log(1.5))), 0.2, 1.5)
    line_ids = draw_line_ids(jax.random.fold_in(key_list[12], 71), 0)
    unit_bus = plant(jax.random.randint(key_list[4], (UNITS,), 0, BUSES // N_AREA), jax.random.fold_in(key_list[4], 1), 0, (BUSES // N_AREA) - 1).astype(jnp.int32)
    node_map = draw_node_map(jax.random.fold_in(key_list[12], 71), 0)
    cost_linear = scatter_about(key_list[6], (UNITS,), 0.5, 3.0, ((0, 16),), jnp.float32)
    cost_quad = jnp.clip(jnp.exp(math.log(2.0) - 1.3862944 * jax.random.uniform(key_list[7], (UNITS,), jnp.float32) ** steps_of(key_list[7], (UNITS,), ((0, 16),), -0.2, 0.2)), 0.5, 2.0)
    capacity = jnp.clip(jnp.exp(math.log(2.0) - 1.3862944 * jax.random.uniform(key_list[8], (UNITS,), jnp.float32) ** steps_of(key_list[8], (UNITS,), ((0, 16),), -0.2, 0.2)), 0.5, 2.0)
    ramp_limits = jnp.clip(jnp.exp(math.log(0.5) - 2.3025851 * jax.random.uniform(key_list[9], (UNITS,), jnp.float32) ** steps_of(key_list[9], (UNITS,), ((0, 16),), -0.2, 0.2)), 0.05, 0.5)
    gen_init = jnp.clip(1.0 * jax.random.uniform(key_list[10], (SCENARIOS, HOURS, UNITS), jnp.float32) ** steps_of(key_list[10], (SCENARIOS, HOURS, UNITS), ((0, 8), (2, 16)), -0.2, 0.2), 0.0, 1.0)
    price_init = scatter_about(key_list[11], (SCENARIOS, HOURS, UNITS), 0.3, 2.0, ((0, 8), (2, 16)), jnp.float32)
    return {"demand": demand, "ptdf": ptdf, "branch_limits": branch_limits, "line_ids": line_ids, "unit_bus": unit_bus, "node_map": node_map, "cost_linear": cost_linear, "cost_quad": cost_quad, "capacity": capacity, "ramp_limits": ramp_limits, "gen_init": gen_init, "price_init": price_init}


def onehot(ids, width):
    return (ids[:, None] == jnp.arange(width, dtype=jnp.int32)[None, :]).astype(jnp.float32)


def node_mean(field, node_map):
    count, hours, units = field.shape
    span = hours // 4
    widths = [1, SECTION2_NODES, SECTION3_NODES, node_map.shape[1] // 2]
    pieces = []
    for section in range(4):
        table = onehot(node_map[section], widths[section])
        block = field[:, section * span:(section + 1) * span, :].reshape(count, span * units)
        totals = jnp.dot(table.T, block, precision=lax.Precision.HIGHEST)
        counts = jnp.maximum(jnp.sum(table, axis=0), 1.0)
        means = jnp.dot(table, totals / counts[:, None], precision=lax.Precision.HIGHEST)
        pieces.append(means.reshape(count, span, units))
    return jnp.concatenate(pieces, axis=1)


def excess(flows, limits):
    return jnp.sign(flows) * jnp.maximum(jnp.abs(flows) - limits, 0.0)


def descend(dispatch, prices, average, demand, ptdf, limits, global_bus, cost_linear, cost_quad, capacity, ramp_limits):
    count, hours, units = dispatch.shape
    buses = ptdf.shape[0]
    power = jnp.zeros((count, hours, buses), jnp.float32).at[:, :, global_bus].add(dispatch)
    injection = (power - demand.astype(jnp.float32)).astype(jnp.bfloat16).reshape(count * hours, buses)
    balance = jnp.sum(injection.astype(jnp.float32), axis=1).reshape(count, hours, 1)
    flows = jnp.dot(injection, ptdf, preferred_element_type=jnp.float32)
    slopes = excess(flows, limits[None, :]).astype(jnp.bfloat16)
    back = lax.dot_general(slopes, ptdf, (((1,), (1,)), ((), ())), preferred_element_type=jnp.float32)
    pull = back[:, global_bus].reshape(count, hours, units)
    change = dispatch[:, 1:, :] - dispatch[:, :-1, :]
    ramp = excess(change, ramp_limits[None, None, :])
    zeros_row = jnp.zeros((count, 1, units), jnp.float32)
    ramp_term = jnp.concatenate([zeros_row, ramp], axis=1) - jnp.concatenate([ramp, zeros_row], axis=1)
    gradient = cost_quad * dispatch + cost_linear + prices + (dispatch - average) + pull + (0.5 / BUSES) * balance + ramp_term
    return jnp.clip(dispatch - 0.25 * gradient, 0.0, capacity)


def reference(demand, ptdf, branch_limits, line_ids, unit_bus, node_map, cost_linear, cost_quad, capacity, ramp_limits, gen_init, price_init):
    unit_area = UNITS // N_AREA
    bus_area = BUSES // N_AREA
    global_bus = (unit_bus + (jnp.arange(UNITS, dtype=jnp.int32) // unit_area) * bus_area).astype(jnp.int32)
    limits = branch_limits[line_ids]
    dispatch = gen_init
    prices = price_init
    average = node_mean(dispatch, node_map)
    for step in range(ITERS):
        dispatch = descend(dispatch, prices, average, demand, ptdf, limits, global_bus, cost_linear, cost_quad, capacity, ramp_limits)
        average = node_mean(dispatch, node_map)
        prices = prices + (dispatch - average)
    return dispatch, prices
```

```python
import functools

import jax
import jax.numpy as jnp
from jax import lax
from jax.experimental import pallas as pl
from jax.experimental.pallas import tpu as pltpu
from jax.sharding import Mesh, PartitionSpec as P

BUSES = 10000
SECTION2_NODES = 4
SECTION3_NODES = 8
ITERS = 2

F32 = jnp.float32
BF16 = jnp.bfloat16
LINES = 2000
LANES = 2048
SCALE_LANE = 2002
BUS_PAD = 640
UNIT_PAD = 256
SPAN = 12
NODE_FIRST = (0, 1, 5)
NODE_WIDTH = (1, SECTION2_NODES, SECTION3_NODES)
ROWS = 32
VMEM = pl.BlockSpec(memory_space=pltpu.VMEM)
SMEM = pl.BlockSpec(memory_space=pltpu.SMEM)
PARAMS = pltpu.CompilerParams(vmem_limit_bytes=56 * 1024 * 1024)


def call(kernel, outs, scratch=()):
    def run(*args):
        specs = [SMEM if a.dtype == jnp.int32 and a.ndim == 1 else VMEM for a in args]
        many = isinstance(outs, (list, tuple))
        return pl.pallas_call(
            kernel,
            out_shape=list(outs) if many else outs,
            in_specs=specs,
            out_specs=[VMEM for _ in outs] if many else VMEM,
            scratch_shapes=list(scratch),
            compiler_params=PARAMS,
        )(*args)

    return run


def shape(dims, dtype):
    return jax.ShapeDtypeStruct(dims, dtype)


def parts3(x):
    hi = x.astype(BF16)
    rest = x - hi.astype(F32)
    mid = rest.astype(BF16)
    low = (rest - mid.astype(F32)).astype(BF16)
    return hi, mid, low


def mm(a, b, dims):
    return lax.dot_general(a, b, (dims, ((), ())), preferred_element_type=F32)


NN = ((1,), (0,))
NT = ((1,), (1,))
TN = ((0,), (0,))


def mm3(a, b, dims):
    return sum(mm(part, b, dims) for part in parts3(a))


def excess(x, limit):
    return x - jnp.minimum(jnp.maximum(x, -limit), limit)


def coded(flows, balance_scale):
    lanes = lax.broadcasted_iota(jnp.int32, flows.shape, 1)
    lines = lanes < LINES
    most = jnp.max(jnp.where(lines, jnp.abs(flows), 0.0), axis=1, keepdims=True)
    power = jnp.floor(14.9 - jnp.log2(jnp.maximum(most, 1e-6)))
    scaled = jnp.where(lines, flows * jnp.exp2(power), 0.0)
    scaled = jnp.where(lanes == LINES, flows * balance_scale, scaled)
    scaled = jnp.where(lanes == SCALE_LANE, power, scaled)
    return jnp.round(scaled).astype(jnp.int32).astype(jnp.int16)


def decoded(code, balance_scale):
    code = code.astype(jnp.int32).astype(F32)
    lanes = lax.broadcasted_iota(jnp.int32, code.shape, 1)
    scale = jnp.exp2(-code[:, SCALE_LANE : SCALE_LANE + 1])
    flows = code * jnp.where(lanes == LINES, 1.0 / balance_scale, scale)
    return jnp.where(lanes > LINES, 0.0, flows)


def prepare_kernel(bus_ref, ptdf_ref, pick_ref, rows_ref):
    rows = lax.broadcasted_iota(jnp.int32, (BUS_PAD, UNIT_PAD), 0)
    pick = (rows == bus_ref[...]).astype(F32).astype(BF16)
    pick_ref[...] = pick
    rows_ref[...] = mm(pick, ptdf_ref[...], TN).astype(BF16)


def limits_kernel(ids_ref, table_ref, out_ref):
    ids = ids_ref[...]
    low = ids & 127
    high = ids >> 7
    lanes = lax.broadcasted_iota(jnp.int32, (128, LANES), 0)
    spread = mm3(table_ref[...], (lanes == low).astype(F32).astype(BF16), NN)
    rows = lax.broadcasted_iota(jnp.int32, spread.shape, 0)
    out_ref[...] = jnp.sum(jnp.where(rows == high, spread, 0.0), axis=0, keepdims=True)


def flows_kernel(
    where_ref,
    own_ref,
    other_ref,
    demand_own_ref,
    demand_other_ref,
    pick_own_ref,
    pick_other_ref,
    ptdf_own_ref,
    ptdf_other_ref,
    *outs,
):
    x, core = where_ref[0], where_ref[2]
    hours, units = other_ref.shape[1:]
    buses = demand_own_ref.shape[2]

    def injected(read_dispatch, read_demand, pick_ref):
        dispatch = jnp.concatenate([read_dispatch(d) for d in range(4)], axis=0)
        demand = jnp.concatenate([read_demand(d) for d in range(4)], axis=0)
        power = mm3(dispatch, pick_ref[...][:, :units], NT)[:, :buses]
        return (power - demand.astype(F32)).astype(BF16)

    def reader(ref, base):
        def read(d):
            first = base + 2 * lax.rem(x + d, 4)
            return ref[pl.ds(first, 2)].astype(F32).reshape(2 * hours, ref.shape[2])

        return read

    own = injected(reader(own_ref, 8 * core), reader(demand_own_ref, 8 * core), pick_own_ref)
    other = injected(reader(other_ref, 0), reader(demand_other_ref, 0), pick_other_ref)
    total = mm(own, ptdf_own_ref[:buses, :], NN) + mm(other, ptdf_other_ref[:buses, :], NN)
    sent = coded(total, 8.0)
    for d in range(4):
        outs[d][...] = sent[d * 2 * hours : (d + 1) * 2 * hours]


def gathered_sum_kernel(where_ref, a_ref, b_ref, c_ref, d_ref, keep_ref, send_ref):
    y = where_ref[1]
    rows = keep_ref.shape[0]

    def total(first):
        cut = slice(first, first + rows)
        return (
            decoded(a_ref[cut, :], 8.0)
            + decoded(b_ref[cut, :], 8.0)
            + decoded(c_ref[cut, :], 8.0)
            + decoded(d_ref[cut, :], 8.0)
        )

    upper, lower = total(0), total(rows)
    keep_ref[...] = jnp.where(y == 0, upper, lower)
    send_ref[...] = coded(jnp.where(y == 0, lower, upper), 4.0)


def slopes_kernel(keep_ref, got_ref, limits_ref, out_ref):
    flows = keep_ref[...] + decoded(got_ref[...], 4.0)
    slopes = excess(flows, limits_ref[...])
    lanes = lax.broadcasted_iota(jnp.int32, flows.shape, 1)
    balance = flows[:, LINES : LINES + 1] * (0.5 / BUSES)
    high = balance.astype(BF16).astype(F32)
    slopes = jnp.where(lanes == LINES, high, slopes)
    slopes = jnp.where(lanes == LINES + 1, balance - high, slopes)
    out_ref[...] = slopes.astype(BF16)


def join_kernel(where_ref, own_ref, got_ref, out_ref):
    y = where_ref[1]
    rows = own_ref.shape[0]

    @pl.when(y == 0)
    def _():
        out_ref[:rows, :] = own_ref[...]
        out_ref[rows:, :] = got_ref[...]

    @pl.when(y != 0)
    def _():
        out_ref[:rows, :] = got_ref[...]
        out_ref[rows:, :] = own_ref[...]


def pull_kernel(where_ref, a_ref, b_ref, c_ref, d_ref, rows_own_ref, rows_other_ref, own_ref, send_ref):
    x = where_ref[0]
    hours = own_ref.shape[1]
    slopes = jnp.concatenate([a_ref[...], b_ref[...], c_ref[...], d_ref[...]], axis=0)
    for rows_ref, out_ref in ((rows_other_ref, send_ref), (rows_own_ref, own_ref)):
        pull = mm(slopes, rows_ref[...], NT)
        for d in range(4):
            first = 2 * lax.rem(x + d, 4)
            block = pull[d * 2 * hours : (d + 1) * 2 * hours]
            out_ref[pl.ds(first, 2)] = block.reshape(2, hours, UNIT_PAD)


def pack_kernel(ids_ref, field_ref, out_ref, wide):
    count, hours, units = field_ref.shape
    wide[...] = jnp.zeros(wide.shape, F32)
    for s in range(count):
        wide[s, :, :units] = field_ref[s, 3 * SPAN :, :]
    for section in range(3):
        cut = slice(section * SPAN, (section + 1) * SPAN)
        for node in range(NODE_WIDTH[section]):
            total = jnp.zeros((SPAN, units), F32)
            for s in range(count):
                inside = ids_ref[section * count + s] == node
                total = total + jnp.where(inside, field_ref[s, cut, :], 0.0)
            wide[count + NODE_FIRST[section] + node, :, :units] = total
    for tile in range(2):
        block = jnp.swapaxes(wide[:, :, tile * 128 : (tile + 1) * 128], 0, 1)
        for hour in range(SPAN):
            out_ref[2 * hour + tile] = block[hour]


def means_kernel(got_ref, leaf_row_ref, leaf_column_ref, counts_ref, out_ref):
    scenarios = leaf_row_ref.shape[1]
    parts = scenarios // 16
    same = leaf_row_ref[...] == leaf_column_ref[...]
    table = same.astype(F32)
    size = jnp.maximum(jnp.sum(table, axis=1, keepdims=True), 1.0)
    table = table.astype(BF16)
    for unit in range(3):
        rows = jnp.concatenate([got_ref[3 * p + unit, :16, :] for p in range(parts)], axis=0)
        leaf = sum(mm(table, part, NN) for part in parts3(rows)) / size
        sums = got_ref[unit, 16:, :]
        for p in range(1, parts):
            sums = sums + got_ref[3 * p + unit, 16:, :]
        node = sums / counts_ref[...]
        for p in range(parts):
            out_ref[3 * p + unit, :16, :] = leaf[16 * p : 16 * (p + 1)]
            out_ref[3 * p + unit, 16:, :] = node


def unpack(ids_ref, means_ref, wide, count):
    for tile in range(2):
        block = jnp.stack([means_ref[2 * hour + tile] for hour in range(SPAN)], axis=0)
        wide[:, :, tile * 128 : (tile + 1) * 128] = jnp.swapaxes(block, 0, 1)

    def average(s, units):
        pieces = []
        for section in range(3):
            row = count + NODE_FIRST[section] + ids_ref[section * count + s]
            pieces.append(wide[row])
        pieces.append(wide[s])
        return jnp.concatenate(pieces, axis=0)[:, :units]

    return average


def gradient_kernel(
    advance,
    where_ref,
    ids_ref,
    dispatch_ref,
    prices_ref,
    means_ref,
    pull_own_ref,
    pull_other_ref,
    quad_ref,
    linear_ref,
    cap_ref,
    ramp_ref,
    out_ref,
    send_ref,
    prices_out_ref,
    wide,
):
    core = where_ref[2]
    count, hours, units = dispatch_ref.shape
    average_of = unpack(ids_ref, means_ref, wide, count)
    zero = jnp.zeros((1, units), F32)

    def one(s, pull):
        dispatch = dispatch_ref[s]
        average = average_of(s, units)
        prices = prices_ref[s]
        if advance:
            prices = prices + (dispatch - average)
        prices_out_ref[s] = prices
        change = jnp.concatenate([dispatch[1:] - dispatch[:-1], zero], axis=0)
        ramp = excess(change, ramp_ref[...])
        ramp_term = jnp.concatenate([zero, ramp[:-1]], axis=0) - ramp
        gradient = (
            quad_ref[...] * dispatch
            + linear_ref[...]
            + prices
            + (dispatch - average)
            + pull[:, :units]
            + ramp_term
        )
        new = jnp.minimum(jnp.maximum(dispatch - 0.25 * gradient, 0.0), cap_ref[...])
        out_ref[s] = new
        return new

    def step(i, carry):
        one(8 * core + i, pull_own_ref[i])
        send_ref[i] = one(8 * (1 - core) + i, pull_other_ref[i])
        return carry

    lax.fori_loop(0, 8, step, 0)


def prices_kernel(ids_ref, dispatch_ref, prices_ref, means_ref, out_ref, wide):
    count, hours, units = dispatch_ref.shape
    average_of = unpack(ids_ref, means_ref, wide, count)

    def step(s, carry):
        out_ref[s] = prices_ref[s] + (dispatch_ref[s] - average_of(s, units))
        return carry

    lax.fori_loop(0, count, step, 0)


def shifted(value, by):
    return lax.ppermute(value, "x", [(i, (i - by) % 4) for i in range(4)])


def swapped(value, axis):
    return lax.ppermute(value, axis, [(0, 1), (1, 0)])


def local(
    demand,
    ptdf,
    branch_limits,
    line_ids,
    unit_bus,
    node_map,
    cost_linear,
    cost_quad,
    capacity,
    ramp_limits,
    gen_init,
    price_init,
):
    count, hours, units = gen_init.shape
    buses = ptdf.shape[0]
    x, y, core = lax.axis_index("x"), lax.axis_index("yhi"), lax.axis_index("core")
    where = jnp.stack([x, y, core]).astype(jnp.int32)
    first = lax.axis_index(("ylo", "z")) * count
    ids = lax.dynamic_slice_in_dim(node_map, first, count, 1).reshape(-1)

    wide_scratch = pltpu.VMEM((ROWS, SPAN, UNIT_PAD), F32)
    flat = (3 * 8, ROWS, 128)
    counts = [
        jnp.sum((node_map[k][None, :] == jnp.arange(w, dtype=jnp.int32)[:, None]).astype(F32), axis=1)
        for k, w in zip(range(3), NODE_WIDTH)
    ]
    counts = jnp.maximum(jnp.concatenate(counts + [jnp.ones((3,), F32)]), 1.0)[:, None]

    def node_means(field):
        packed = call(pack_kernel, shape(flat, F32), [wide_scratch])(ids, field)
        got = lax.all_to_all(packed, ("ylo", "z"), 0, 0, tiled=True)
        means = call(means_kernel, shape(flat, F32))(
            got, node_map[3][None, :], node_map[3][:, None], counts
        )
        return lax.all_to_all(means, ("ylo", "z"), 0, 0, tiled=True)

    def other_half(field):
        return lax.dynamic_slice_in_dim(field, 8 * (1 - core), 8, 0)

    ptdf_other = swapped(ptdf, "core")
    bus_other = swapped(unit_bus.astype(F32), "core").astype(jnp.int32)
    demand_other = swapped(other_half(demand), "core")
    dispatch_other = swapped(other_half(gen_init), "core")

    def padded(table):
        wide = jnp.pad(table, ((0, BUS_PAD - buses), (0, LANES - LINES)))
        lane = lax.broadcasted_iota(jnp.int32, wide.shape, 1)
        return jnp.where((lane == LINES) | (lane == LINES + 1), jnp.ones((), BF16), wide)

    def prepared(bus, table):
        row = jnp.pad(bus, (0, UNIT_PAD - units), constant_values=-1)[None, :]
        return call(
            prepare_kernel,
            [shape((BUS_PAD, UNIT_PAD), BF16), shape((UNIT_PAD, LANES), BF16)],
        )(row, table)

    ptdf_own, ptdf_other = padded(ptdf), padded(ptdf_other)
    pick_own, rows_own = prepared(unit_bus, ptdf_own)
    pick_other, rows_other = prepared(bus_other, ptdf_other)
    table = jnp.pad(branch_limits, (0, 96 * 128 - branch_limits.shape[0])).reshape(96, 128)
    limits = call(limits_kernel, shape((1, LANES), F32))(
        jnp.pad(line_ids, (0, LANES - LINES))[None, :], table
    )

    block = (2 * hours, LANES)
    part = (hours, LANES)
    half = (8, hours, UNIT_PAD)

    dispatch, prices = gen_init, price_init
    for step in range(ITERS):
        sums = call(flows_kernel, [shape(block, jnp.int16)] * 4)(
            where,
            dispatch,
            dispatch_other,
            demand,
            demand_other,
            pick_own,
            pick_other,
            ptdf_own,
            ptdf_other,
        )
        got = [shifted(sums[d], -d) for d in (1, 2, 3)]
        means = node_means(dispatch)
        keep, send = call(gathered_sum_kernel, [shape(part, F32), shape(part, jnp.int16)])(
            where, sums[0], *got
        )
        slopes = call(slopes_kernel, shape(part, BF16))(keep, swapped(send, "yhi"), limits)
        own = call(join_kernel, shape(block, BF16))(where, slopes, swapped(slopes, "yhi"))
        blocks = [own] + [shifted(own, d) for d in (1, 2, 3)]
        pull_own, pull_send = call(pull_kernel, [shape(half, F32)] * 2)(
            where, *blocks, rows_own, rows_other
        )
        pull_other = swapped(pull_send, "core")
        dispatch, send, prices = call(
            functools.partial(gradient_kernel, step > 0),
            [
                shape((count, hours, units), F32),
                shape((8, hours, units), F32),
                shape((count, hours, units), F32),
            ],
            [wide_scratch],
        )(
            where,
            ids,
            dispatch,
            prices,
            means,
            pull_own,
            pull_other,
            cost_quad[None, :],
            cost_linear[None, :],
            capacity[None, :],
            ramp_limits[None, :],
        )
        if step + 1 < ITERS:
            dispatch_other = swapped(send, "core")
    means = node_means(dispatch)
    prices = call(prices_kernel, shape((count, hours, units), F32), [wide_scratch])(
        ids, dispatch, prices, means
    )
    return (dispatch, prices)


def solution(mesh):
    fine = Mesh(mesh.devices.reshape(2, 4, 2, 4, 2), ("ylo", "z", "yhi", "x", "core"))
    scen, area = ("ylo", "z"), ("yhi", "x", "core")
    return jax.shard_map(
        local,
        mesh=fine,
        in_specs=(
            P(scen, None, area),
            P(area, None),
            P(),
            P(),
            P(area),
            P(),
            P(area),
            P(area),
            P(area),
            P(area),
            P(scen, None, area),
            P(scen, None, area),
        ),
        out_specs=(P(scen, None, area), P(scen, None, area)),
        check_vma=False,
    )
```

```python
import functools

import jax
import jax.numpy as jnp
from jax import lax
from jax.experimental import pallas as pl
from jax.experimental.pallas import tpu as pltpu
from jax.sharding import Mesh, PartitionSpec as P

BUSES = 10000
SECTION2_NODES = 4
SECTION3_NODES = 8
ITERS = 2

F32 = jnp.float32
BF16 = jnp.bfloat16
LINES = 2000
LANES = 2048
BALANCE_SCALE = 8.0
UNIT_PAD = 256
SPAN = 12
NODE_FIRST = (0, 1, 5)
NODE_WIDTH = (1, SECTION2_NODES, SECTION3_NODES)
SENDS = (6, 5, 7, 2, 4, 1, 3)
ROWS = 32
VMEM = pl.BlockSpec(memory_space=pltpu.VMEM)
SMEM = pl.BlockSpec(memory_space=pltpu.SMEM)
PARAMS = pltpu.CompilerParams(vmem_limit_bytes=56 * 1024 * 1024)


def call(kernel, outs, scratch=(), after=0):
    def run(*args):
        specs = [SMEM if a.dtype == jnp.int32 and a.ndim == 1 else VMEM for a in args]
        if after:
            specs[-after:] = [pl.BlockSpec(memory_space=pl.ANY)] * after
        many = isinstance(outs, (list, tuple))
        return pl.pallas_call(
            kernel,
            out_shape=list(outs) if many else outs,
            in_specs=specs,
            out_specs=[VMEM for _ in outs] if many else VMEM,
            scratch_shapes=list(scratch),
            compiler_params=PARAMS,
        )(*args)

    return run


def shape(dims, dtype):
    return jax.ShapeDtypeStruct(dims, dtype)


def parts3(x):
    hi = x.astype(BF16)
    rest = x - hi.astype(F32)
    mid = rest.astype(BF16)
    low = (rest - mid.astype(F32)).astype(BF16)
    return hi, mid, low


def mm(a, b, dims):
    return lax.dot_general(a, b, (dims, ((), ())), preferred_element_type=F32)


NN = ((1,), (0,))
NT = ((1,), (1,))
TN = ((0,), (0,))


def mm3(a, b, dims):
    return sum(mm(part, b, dims) for part in parts3(a))


def excess(x, limit):
    return x - jnp.minimum(jnp.maximum(x, -limit), limit)


def prepare_kernel(bus_ref, ptdf_ref, pick_ref, rows_ref):
    buses, units = pick_ref.shape
    rows = lax.broadcasted_iota(jnp.int32, (buses, units), 0)
    pick = (rows == bus_ref[...]).astype(F32).astype(BF16)
    pick_ref[...] = pick
    rows_ref[:LINES, :] = mm(ptdf_ref[...], pick, NN).astype(BF16)
    spare = lax.broadcasted_iota(jnp.int32, (LANES - LINES, units), 0) < 2
    rows_ref[LINES:, :] = spare.astype(F32).astype(BF16)


def limits_kernel(ids_ref, table_ref, out_ref):
    ids = ids_ref[...]
    low = ids & 127
    high = ids >> 7
    lanes = lax.broadcasted_iota(jnp.int32, (128, LANES), 0)
    spread = mm3(table_ref[...], (lanes == low).astype(F32).astype(BF16), NN)
    rows = lax.broadcasted_iota(jnp.int32, spread.shape, 0)
    out_ref[...] = jnp.sum(jnp.where(rows == high, spread, 0.0), axis=0, keepdims=True)


def flows_kernel(
    where_ref,
    own_ref,
    other_ref,
    demand_own_ref,
    demand_other_ref,
    pick_own_ref,
    pick_other_ref,
    ptdf_own_ref,
    ptdf_other_ref,
    *outs,
):
    x, y, core = where_ref[0], where_ref[1], where_ref[2]
    hours = other_ref.shape[1]
    order = [4 * lax.rem(y + r // 4, 2) + lax.rem(x + r % 4, 4) for r in range(8)]

    def injected(dispatch_ref, demand_ref, pick_ref):
        first = 8 * core if dispatch_ref.shape[0] > 8 else 0
        dispatch = jnp.concatenate([dispatch_ref[first + s] for s in order], axis=0)
        demand = jnp.concatenate([demand_ref[8 * core + s].astype(F32) for s in order], axis=0)
        power = mm3(dispatch, pick_ref[...], NT)
        return (power - demand).astype(BF16)

    own = injected(own_ref, demand_own_ref, pick_own_ref)
    other = injected(other_ref, demand_other_ref, pick_other_ref)
    balance = jnp.sum(own.astype(F32), axis=1, keepdims=True)
    balance = balance + jnp.sum(other.astype(F32), axis=1, keepdims=True)
    total = mm(own, ptdf_own_ref[...], NT) + mm(other, ptdf_other_ref[...], NT)
    most = jnp.max(jnp.abs(total), axis=1, keepdims=True)
    power = jnp.floor(14.9 - jnp.log2(jnp.maximum(most, 1e-6)))
    code = total * jnp.exp2(power)
    lanes = lax.broadcasted_iota(jnp.int32, (code.shape[0], LANES - LINES), 1)
    spare = jnp.where(lanes == 0, balance * BALANCE_SCALE, jnp.where(lanes == 1, power, 0.0))
    code = jnp.concatenate([code, spare], axis=1)
    code = jnp.round(code).astype(jnp.int32).astype(jnp.int16)
    for r in range(8):
        outs[r][...] = code[r * hours : (r + 1) * hours]


def slopes_kernel(*refs):
    codes, limits_ref, out_ref = refs[:8], refs[8], refs[-1]
    lanes = lax.broadcasted_iota(jnp.int32, out_ref.shape, 1)
    flows = jnp.zeros(out_ref.shape, F32)
    for ref in codes:
        code = ref[...].astype(jnp.int32).astype(F32)
        scale = jnp.exp2(-code[:, LINES + 1 : LINES + 2])
        flows = flows + code * jnp.where(lanes == LINES, 1.0 / BALANCE_SCALE, scale)
    slopes = excess(flows, limits_ref[...])
    balance = flows[:, LINES : LINES + 1] * (0.5 / BUSES)
    high = balance.astype(BF16).astype(F32)
    slopes = jnp.where(lanes == LINES, high, slopes)
    slopes = jnp.where(lanes == LINES + 1, balance - high, slopes)
    out_ref[...] = jnp.where(lanes > LINES + 1, 0.0, slopes).astype(BF16)


def pull_kernel(where_ref, *refs):
    blocks, (rows_own_ref, rows_other_ref), (own_ref, send_ref) = refs[:8], refs[8:10], refs[-2:]
    x, y = where_ref[0], where_ref[1]
    hours = own_ref.shape[1]
    slopes = jnp.concatenate([ref[...] for ref in blocks], axis=0)
    for rows_ref, out_ref in ((rows_other_ref, send_ref), (rows_own_ref, own_ref)):
        pull = mm(slopes, rows_ref[...], NN)
        for r in range(8):
            s = 4 * lax.rem(y + r // 4, 2) + lax.rem(x + r % 4, 4)
            out_ref[s] = pull[r * hours : (r + 1) * hours]


def pack_kernel(ids_ref, field_ref, out_ref, wide):
    count, hours, units = field_ref.shape
    wide[...] = jnp.zeros(wide.shape, F32)
    for s in range(count):
        wide[s, :, :units] = field_ref[s, 3 * SPAN :, :]
    for section in range(3):
        cut = slice(section * SPAN, (section + 1) * SPAN)
        for node in range(NODE_WIDTH[section]):
            total = jnp.zeros((SPAN, units), F32)
            for s in range(count):
                inside = ids_ref[section * count + s] == node
                total = total + jnp.where(inside, field_ref[s, cut, :], 0.0)
            wide[count + NODE_FIRST[section] + node, :, :units] = total
    for tile in range(2):
        block = jnp.swapaxes(wide[:, :, tile * 128 : (tile + 1) * 128], 0, 1)
        for hour in range(SPAN):
            out_ref[2 * hour + tile] = block[hour]


def means_kernel(got_ref, leaf_row_ref, leaf_column_ref, counts_ref, out_ref):
    scenarios = leaf_row_ref.shape[1]
    parts = scenarios // 16
    same = leaf_row_ref[...] == leaf_column_ref[...]
    table = same.astype(F32)
    size = jnp.maximum(jnp.sum(table, axis=1, keepdims=True), 1.0)
    table = table.astype(BF16)
    for unit in range(3):
        rows = jnp.concatenate([got_ref[3 * p + unit, :16, :] for p in range(parts)], axis=0)
        leaf = sum(mm(table, part, NN) for part in parts3(rows)) / size
        sums = got_ref[unit, 16:, :]
        for p in range(1, parts):
            sums = sums + got_ref[3 * p + unit, 16:, :]
        node = sums / counts_ref[...]
        for p in range(parts):
            out_ref[3 * p + unit, :16, :] = leaf[16 * p : 16 * (p + 1)]
            out_ref[3 * p + unit, 16:, :] = node


def unpack(ids_ref, means_ref, wide, count):
    for tile in range(2):
        block = jnp.stack([means_ref[2 * hour + tile] for hour in range(SPAN)], axis=0)
        wide[:, :, tile * 128 : (tile + 1) * 128] = jnp.swapaxes(block, 0, 1)

    def average(s, units):
        pieces = []
        for section in range(3):
            row = count + NODE_FIRST[section] + ids_ref[section * count + s]
            pieces.append(wide[row])
        pieces.append(wide[s])
        return jnp.concatenate(pieces, axis=0)[:, :units]

    return average


def gradient_kernel(
    advance,
    where_ref,
    ids_ref,
    dispatch_ref,
    prices_ref,
    means_ref,
    pull_own_ref,
    pull_other_ref,
    quad_ref,
    linear_ref,
    cap_ref,
    ramp_ref,
    out_ref,
    send_ref,
    prices_out_ref,
    wide,
):
    core = where_ref[2]
    count, hours, units = dispatch_ref.shape
    average_of = unpack(ids_ref, means_ref, wide, count)
    zero = jnp.zeros((1, units), F32)

    def one(s, pull):
        dispatch = dispatch_ref[s]
        average = average_of(s, units)
        prices = prices_ref[s]
        if advance:
            prices = prices + (dispatch - average)
        prices_out_ref[s] = prices
        change = jnp.concatenate([dispatch[1:] - dispatch[:-1], zero], axis=0)
        ramp = excess(change, ramp_ref[...])
        ramp_term = jnp.concatenate([zero, ramp[:-1]], axis=0) - ramp
        gradient = (
            quad_ref[...] * dispatch
            + linear_ref[...]
            + prices
            + (dispatch - average)
            + pull
            + ramp_term
        )
        new = jnp.minimum(jnp.maximum(dispatch - 0.25 * gradient, 0.0), cap_ref[...])
        out_ref[s] = new
        return new

    def step(i, carry):
        one(8 * core + i, pull_own_ref[i])
        send_ref[i] = one(8 * (1 - core) + i, pull_other_ref[i])
        return carry

    lax.fori_loop(0, 8, step, 0)


def prices_kernel(ids_ref, dispatch_ref, prices_ref, means_ref, out_ref, wide):
    count, hours, units = dispatch_ref.shape
    average_of = unpack(ids_ref, means_ref, wide, count)

    def step(s, carry):
        out_ref[s] = prices_ref[s] + (dispatch_ref[s] - average_of(s, units))
        return carry

    lax.fori_loop(0, count, step, 0)


def sent_to(value, r):
    pairs = [(y * 4 + x, (y + r // 4) % 2 * 4 + (x + r % 4) % 4) for y in range(2) for x in range(4)]
    return lax.ppermute(value, ("yhi", "x"), pairs)


def swapped(value):
    return lax.ppermute(value, "core", [(0, 1), (1, 0)])


def local(
    demand,
    ptdf,
    branch_limits,
    line_ids,
    unit_bus,
    node_map,
    cost_linear,
    cost_quad,
    capacity,
    ramp_limits,
    gen_init,
    price_init,
):
    count, hours, units = gen_init.shape
    buses = ptdf.shape[0]
    x, y, core = lax.axis_index("x"), lax.axis_index("yhi"), lax.axis_index("core")
    where = jnp.stack([x, y, core]).astype(jnp.int32)
    first = lax.axis_index(("ylo", "z")) * count
    ids = lax.dynamic_slice_in_dim(node_map, first, count, 1).reshape(-1)

    wide_scratch = pltpu.VMEM((ROWS, SPAN, UNIT_PAD), F32)
    flat = (3 * 8, ROWS, 128)
    counts = [
        jnp.sum((node_map[k][None, :] == jnp.arange(w, dtype=jnp.int32)[:, None]).astype(F32), axis=1)
        for k, w in zip(range(3), NODE_WIDTH)
    ]
    counts = jnp.maximum(jnp.concatenate(counts + [jnp.ones((3,), F32)]), 1.0)[:, None]

    def packed(field):
        sums = call(pack_kernel, shape(flat, F32), [wide_scratch])(ids, field)
        return lax.all_to_all(sums, ("ylo", "z"), 0, 0, tiled=True)

    def meaned(sums):
        return call(means_kernel, shape(flat, F32))(sums, node_map[3][None, :], node_map[3][:, None], counts)

    def returned(means):
        return lax.all_to_all(means, ("ylo", "z"), 0, 0, tiled=True)

    lines = ptdf.T
    lines_other = swapped(lines)
    bus_other = swapped(unit_bus)
    demand_other = swapped(demand)
    dispatch_other = swapped(gen_init)

    prepared = call(prepare_kernel, [shape((buses, units), BF16), shape((LANES, units), BF16)])
    pick_own, rows_own = prepared(unit_bus[None, :], lines)
    pick_other, rows_other = prepared(bus_other[None, :], lines_other)
    table = jnp.pad(branch_limits, (0, 96 * 128 - branch_limits.shape[0])).reshape(96, 128)
    limits = call(limits_kernel, shape((1, LANES), F32))(
        jnp.pad(line_ids, (0, LANES - LINES))[None, :], table
    )

    block = (hours, LANES)
    half = (8, hours, units)
    whole = (count, hours, units)

    dispatch, prices = gen_init, price_init
    for step in range(ITERS):
        codes = call(flows_kernel, [shape(block, jnp.int16)] * 8)(
            where,
            dispatch,
            dispatch_other,
            demand,
            demand_other,
            pick_own,
            pick_other,
            lines,
            lines_other,
        )
        got = [sent_to(codes[r], r) for r in SENDS]
        means = meaned(packed(dispatch))
        slopes = call(slopes_kernel, shape(block, BF16), after=1)(codes[0], *got, limits, means)
        means = returned(means)
        blocks = {r: sent_to(slopes, (r // 4) * 4 + (4 - r % 4) % 4) for r in SENDS}
        pull_own, pull_send = call(pull_kernel, [shape(half, F32)] * 2, after=1)(
            where, slopes, *[blocks[r] for r in range(1, 8)], rows_own, rows_other, means
        )
        pull_other = swapped(pull_send)
        dispatch, send, prices = call(
            functools.partial(gradient_kernel, step > 0),
            [shape(whole, F32), shape(half, F32), shape(whole, F32)],
            [wide_scratch],
        )(
            where,
            ids,
            dispatch,
            prices,
            means,
            pull_own,
            pull_other,
            cost_quad[None, :],
            cost_linear[None, :],
            capacity[None, :],
            ramp_limits[None, :],
        )
        if step + 1 < ITERS:
            dispatch_other = swapped(send)
    means = returned(meaned(packed(dispatch)))
    prices = call(prices_kernel, shape(whole, F32), [wide_scratch])(ids, dispatch, prices, means)
    return (dispatch, prices)


def solution(mesh):
    fine = Mesh(mesh.devices.reshape(2, 4, 2, 4, 2), ("ylo", "z", "yhi", "x", "core"))
    scen, area = ("ylo", "z"), ("yhi", "x", "core")
    return jax.shard_map(
        local,
        mesh=fine,
        in_specs=(
            P(scen, None, area),
            P(area, None),
            P(),
            P(),
            P(area),
            P(),
            P(area),
            P(area),
            P(area),
            P(area),
            P(scen, None, area),
            P(scen, None, area),
        ),
        out_specs=(P(scen, None, area), P(scen, None, area)),
        check_vma=False,
    )
```

```python
import functools

import jax
import jax.numpy as jnp
from jax import lax
from jax.experimental import pallas as pl
from jax.experimental.pallas import tpu as pltpu
from jax.sharding import Mesh, PartitionSpec as P

BUSES = 10000
SECTION2_NODES = 4
SECTION3_NODES = 8
ITERS = 2

F32 = jnp.float32
BF16 = jnp.bfloat16
LINES = 2000
LANES = 2048
WIDTH = 512
BALANCE_SCALE = 8.0
UNIT_PAD = 256
SPAN = 12
NODE_FIRST = (0, 1, 5)
NODE_WIDTH = (1, SECTION2_NODES, SECTION3_NODES)
VALUE_SCALE = 16383.0
SUM_SCALE = 1023.0
VMEM = pl.BlockSpec(memory_space=pltpu.VMEM)
SMEM = pl.BlockSpec(memory_space=pltpu.SMEM)
PARAMS = pltpu.CompilerParams(vmem_limit_bytes=56 * 1024 * 1024)


def call(kernel, outs, scratch=(), after=0, large=(), out=VMEM):
    def run(*args):
        specs = [SMEM if a.dtype == jnp.int32 and a.ndim == 1 else VMEM for a in args]
        for i in large:
            specs[i] = pl.BlockSpec(memory_space=pl.ANY)
        if after:
            specs[-after:] = [pl.BlockSpec(memory_space=pl.ANY)] * after
        many = isinstance(outs, (list, tuple))
        return pl.pallas_call(
            kernel,
            out_shape=list(outs) if many else outs,
            in_specs=specs,
            out_specs=[out for _ in outs] if many else out,
            scratch_shapes=list(scratch),
            compiler_params=PARAMS,
        )(*args)

    return run


def shape(dims, dtype):
    return jax.ShapeDtypeStruct(dims, dtype)


def parts3(x):
    hi = x.astype(BF16)
    rest = x - hi.astype(F32)
    mid = rest.astype(BF16)
    low = (rest - mid.astype(F32)).astype(BF16)
    return hi, mid, low


def mm(a, b, dims):
    return lax.dot_general(a, b, (dims, ((), ())), preferred_element_type=F32)


NN = ((1,), (0,))
NT = ((1,), (1,))
TN = ((0,), (0,))


def mm3(a, b, dims):
    return sum(mm(part, b, dims) for part in parts3(a))


def excess(x, limit):
    return x - jnp.minimum(jnp.maximum(x, -limit), limit)


def pick(bus_ref, buses):
    rows = lax.broadcasted_iota(jnp.int32, (buses, bus_ref.shape[1]), 0)
    return (rows == bus_ref[...]).astype(F32).astype(BF16)


def unit_rows_kernel(bus_ref, ptdf_ref, _, out_ref):
    out_ref[:LINES, :] = mm(ptdf_ref[...], pick(bus_ref, ptdf_ref.shape[1]), NN).astype(BF16)
    spare = lax.broadcasted_iota(jnp.int32, (LANES - LINES, out_ref.shape[1]), 0) < 2
    out_ref[LINES:, :] = spare.astype(F32).astype(BF16)


def limits_kernel(ids_ref, table_ref, _, out_ref):
    ids = ids_ref[...]
    low = ids & 127
    high = ids >> 7
    lanes = lax.broadcasted_iota(jnp.int32, (128, LANES), 0)
    spread = mm3(table_ref[...], (lanes == low).astype(F32).astype(BF16), NN)
    rows = lax.broadcasted_iota(jnp.int32, spread.shape, 0)
    out_ref[...] = jnp.sum(jnp.where(rows == high, spread, 0.0), axis=0, keepdims=True)


def flows_kernel(
    where_ref,
    own_ref,
    other_ref,
    bus_own_ref,
    bus_other_ref,
    demand_own_ref,
    demand_other_ref,
    ptdf_own_ref,
    ptdf_other_ref,
    *rest,
):
    out_ref, demand, ptdf, sems = rest[-4:]
    core = where_ref[2]
    hours = other_ref.shape[1]
    buses = demand.shape[3]
    rows = 8 * hours
    copies = [
        pltpu.make_async_copy(demand_own_ref.at[pl.ds(8 * core, 8)], demand.at[0], sems.at[0]),
        pltpu.make_async_copy(demand_other_ref.at[pl.ds(8 * core, 8)], demand.at[1], sems.at[1]),
        pltpu.make_async_copy(ptdf_own_ref, ptdf.at[0], sems.at[2]),
        pltpu.make_async_copy(ptdf_other_ref, ptdf.at[1], sems.at[3]),
    ]
    for copy in copies:
        copy.start()

    def injected(i, dispatch_ref, bus_ref):
        first = 8 * core if dispatch_ref.shape[0] > 8 else 0
        dispatch = dispatch_ref[pl.ds(first, 8)].reshape(rows, dispatch_ref.shape[2])
        power = mm3(dispatch, pick(bus_ref, buses), NT)
        copies[i].wait()
        load = demand[i].astype(F32).reshape(rows, buses)
        return (power - load).astype(BF16)

    own = injected(0, own_ref, bus_own_ref)
    other = injected(1, other_ref, bus_other_ref)
    balance = jnp.sum(own.astype(F32), axis=1, keepdims=True)
    balance = balance + jnp.sum(other.astype(F32), axis=1, keepdims=True)
    copies[2].wait()
    copies[3].wait()
    lanes = lax.broadcasted_iota(jnp.int32, (own.shape[0], LANES - LINES), 1)
    spare = jnp.where(lanes == 0, balance * BALANCE_SCALE, 0.0)
    for tile in range(LANES // WIDTH):
        lines = slice(tile * WIDTH, min((tile + 1) * WIDTH, LINES))
        total = mm(own, ptdf[0, lines, :], NT) + mm(other, ptdf[1, lines, :], NT)
        most = jnp.max(jnp.abs(total), axis=1, keepdims=True)
        power = jnp.floor(14.9 - jnp.log2(jnp.maximum(most, 1e-6)))
        code = total * jnp.exp2(power)
        spare = jnp.where(lanes == 1 + tile, power, spare)
        if lines.stop == LINES:
            code = jnp.concatenate([code, spare], axis=1)
        code = jnp.round(code).astype(jnp.int32).astype(jnp.int16)
        for r in range(8):
            out_ref[r, :, tile * WIDTH : (tile + 1) * WIDTH] = code[r * hours : (r + 1) * hours]


def slopes_kernel(codes_ref, limits_ref, *rest):
    out_ref = rest[-1]
    rows = out_ref.shape[1]
    tiles = LANES // WIDTH
    lanes = lax.broadcasted_iota(jnp.int32, (rows, WIDTH), 1) + (LANES - WIDTH)
    last = LANES - WIDTH
    spare = [codes_ref[r, :, last:].astype(jnp.int32).astype(F32)[:, LINES - last :] for r in range(8)]
    for tile in range(tiles):
        cut = slice(tile * WIDTH, (tile + 1) * WIDTH)
        flows = jnp.zeros((rows, WIDTH), F32)
        for r in range(8):
            code = codes_ref[r, :, cut].astype(jnp.int32).astype(F32)
            flows = flows + code * jnp.exp2(-spare[r][:, 1 + tile : 2 + tile])
        slopes = excess(flows, limits_ref[:, cut])
        if tile == tiles - 1:
            balance = sum(part[:, :1] for part in spare) * (0.5 / BUSES / BALANCE_SCALE)
            high = balance.astype(BF16).astype(F32)
            slopes = jnp.where(lanes == LINES, high, slopes)
            slopes = jnp.where(lanes == LINES + 1, balance - high, slopes)
            slopes = jnp.where(lanes > LINES + 1, 0.0, slopes)
        slopes = slopes.astype(BF16)
        for r in range(8):
            out_ref[r, :, cut] = slopes


def ids_kernel(count, where_ref, flat_ref, map_ref, out_ref):
    scenarios = map_ref.shape[1]
    ylo, z = where_ref[0], where_ref[1]
    first = (4 * ylo + z) * count
    lanes = lax.broadcasted_iota(jnp.int32, (1, scenarios), 1)
    holder = lanes // count
    place = (2 * ((holder - z) & 3) + (((holder >> 2) - ylo) & 1)) * count + (lanes & (count - 1))
    for s in range(count):
        for section in range(3):
            out_ref[section * count + s] = flat_ref[section * scenarios + first + s]
        leaf = flat_ref[3 * scenarios + first + s]
        paired = (map_ref[3:4, :] == leaf) & (lanes != first + s)
        out_ref[3 * count + s] = jnp.max(jnp.where(paired, place, 0))
    row = 4 * count
    for section in range(3):
        for node in range(NODE_WIDTH[section]):
            inside = (map_ref[section : section + 1, :] == node).astype(jnp.int32)
            out_ref[row] = jnp.maximum(jnp.sum(inside), 1)
            row += 1
    for rest in range(row, 5 * count):
        out_ref[rest] = 0


def folded(x):
    x = jnp.concatenate([x, jnp.zeros((SPAN, UNIT_PAD - x.shape[1]), F32)], axis=1)
    return jnp.concatenate([x[:, :128], x[:, 128:]], axis=0)


def unfolded(x, units):
    return jnp.concatenate([x[:SPAN], x[SPAN:]], axis=1)[:, :units]


def fixed(x, scale):
    code = jnp.round(x * scale).astype(jnp.int32)
    return jnp.minimum(jnp.maximum(code, -32767), 32767).astype(jnp.int16)


def pack_kernel(ids_ref, field_ref, out_ref):
    count = field_ref.shape[0]
    for s in range(count):
        out_ref[s] = fixed(folded(field_ref[s, 3 * SPAN :, :]), VALUE_SCALE)
    for section in range(3):
        cut = slice(section * SPAN, (section + 1) * SPAN)
        fields = [field_ref[s, cut, :] for s in range(count)]
        for node in range(NODE_WIDTH[section]):
            total = jnp.zeros(fields[0].shape, F32)
            for s in range(count):
                inside = ids_ref[section * count + s] == node
                total = total + jnp.where(inside, fields[s], 0.0)
            out_ref[count + NODE_FIRST[section] + node] = fixed(folded(total), SUM_SCALE)


def join_kernel(own_ref, got_ref, out_ref):
    count = own_ref.shape[0] - sum(NODE_WIDTH)
    out_ref[:count] = own_ref[:count]
    out_ref[count : 2 * count] = got_ref[:count]
    for node in range(sum(NODE_WIDTH)):
        total = own_ref[count + node].astype(jnp.int32) + got_ref[count + node].astype(jnp.int32)
        if node < NODE_FIRST[2]:
            total = jnp.round(total.astype(F32) * 0.5).astype(jnp.int32)
        out_ref[2 * count + node] = total.astype(jnp.int16)


def unpack(ids_ref, got_refs, rows, means, count, units):
    for i, ref in enumerate(got_refs):
        rows[2 * i * count : 2 * (i + 1) * count] = ref[: 2 * count]
    for node in range(sum(NODE_WIDTH)):
        total = jnp.zeros((2 * SPAN, 128), F32)
        for ref in got_refs:
            total = total + ref[2 * count + node].astype(jnp.int32).astype(F32)
        scale = SUM_SCALE if node >= NODE_FIRST[2] else SUM_SCALE / 2
        size = ids_ref[4 * count + node].astype(F32)
        means[node] = unfolded(total * (1.0 / scale) / size, units)

    def average(s, dispatch):
        pieces = [means[NODE_FIRST[k] + ids_ref[k * count + s]] for k in range(3)]
        partner = rows[ids_ref[3 * count + s]].astype(jnp.int32).astype(F32)
        partner = unfolded(partner, units) * (1.0 / VALUE_SCALE)
        pieces.append((dispatch[3 * SPAN :] + partner) * 0.5)
        return jnp.concatenate(pieces, axis=0)

    return average


def gradient_kernel(
    advance,
    where_ref,
    ids_ref,
    dispatch_ref,
    prices_ref,
    pull_own_ref,
    pull_other_ref,
    quad_ref,
    linear_ref,
    cap_ref,
    ramp_ref,
    *rest,
):
    got_refs, (out_ref, send_ref, prices_out_ref, rows, means) = rest[:4], rest[4:]
    core = where_ref[2]
    count, hours, units = dispatch_ref.shape
    average_of = unpack(ids_ref, got_refs, rows, means, count, units)
    zero = jnp.zeros((1, units), F32)

    def one(s, pull):
        dispatch = dispatch_ref[s]
        average = average_of(s, dispatch)
        prices = prices_ref[s]
        if advance:
            prices = prices + (dispatch - average)
        prices_out_ref[s] = prices
        change = jnp.concatenate([dispatch[1:] - dispatch[:-1], zero], axis=0)
        ramp = excess(change, ramp_ref[...])
        ramp_term = jnp.concatenate([zero, ramp[:-1]], axis=0) - ramp
        gradient = (
            quad_ref[...] * dispatch
            + linear_ref[...]
            + prices
            + (dispatch - average)
            + pull
            + ramp_term
        )
        new = jnp.minimum(jnp.maximum(dispatch - 0.25 * gradient, 0.0), cap_ref[...])
        out_ref[s] = new
        return new

    def step(i, carry):
        one(8 * core + i, pull_own_ref[i])
        send_ref[i] = one(8 * (1 - core) + i, pull_other_ref[i])
        return carry

    lax.fori_loop(0, 8, step, 0)


def prices_kernel(ids_ref, dispatch_ref, prices_ref, *rest):
    got_refs, (out_ref, rows, means) = rest[:4], rest[4:]
    count, hours, units = dispatch_ref.shape
    average_of = unpack(ids_ref, got_refs, rows, means, count, units)

    def step(s, carry):
        dispatch = dispatch_ref[s]
        out_ref[s] = prices_ref[s] + (dispatch - average_of(s, dispatch))
        return carry

    lax.fori_loop(0, count, step, 0)


def swapped(value, axis="core"):
    return lax.ppermute(value, axis, [(0, 1), (1, 0)])


def exchanged(blocks):
    return lax.all_to_all(blocks, ("yhi", "x"), 0, 0, tiled=True)


def local(
    demand,
    ptdf,
    branch_limits,
    line_ids,
    unit_bus,
    node_map,
    cost_linear,
    cost_quad,
    capacity,
    ramp_limits,
    gen_init,
    price_init,
):
    count, hours, units = gen_init.shape
    buses = ptdf.shape[0]
    x, y, core = lax.axis_index("x"), lax.axis_index("yhi"), lax.axis_index("core")
    where = jnp.stack([x, y, core]).astype(jnp.int32)
    ylo, z = lax.axis_index("ylo"), lax.axis_index("z")
    ids = call(
        functools.partial(ids_kernel, count),
        shape((5 * count,), jnp.int32),
        out=SMEM,
    )(jnp.stack([ylo, z]).astype(jnp.int32), node_map.reshape(-1), node_map)

    payload = (count + sum(NODE_WIDTH), 2 * SPAN, 128)
    unpacking = [
        pltpu.VMEM((node_map.shape[1],) + payload[1:], jnp.int16),
        pltpu.VMEM((sum(NODE_WIDTH), SPAN, units), F32),
    ]

    def packed(field):
        return call(pack_kernel, shape(payload, jnp.int16))(ids, field)

    def joined(own, beside):
        both = (2 * count + sum(NODE_WIDTH),) + payload[1:]
        return call(join_kernel, shape(both, jnp.int16))(own, beside)

    def gathered(pair):
        return [pair] + [lax.ppermute(pair, "z", [(i, (i - d) % 4) for i in range(4)]) for d in (1, 2, 3)]

    lines = ptdf.T
    lines_other = swapped(lines)
    bus_other = swapped(unit_bus)
    demand_other = swapped(demand)
    dispatch_other = swapped(gen_init)

    bus_own, bus_other = unit_bus[None, :], bus_other[None, :]
    table = jnp.pad(branch_limits, (0, 96 * 128 - branch_limits.shape[0])).reshape(96, 128)
    block = (8, hours, LANES)
    half = (8, hours, units)
    whole = (count, hours, units)

    def pulled(slopes, rows):
        pull = jnp.dot(slopes.reshape(8 * hours, LANES), rows, preferred_element_type=F32)
        return pull.reshape(half)

    dispatch, prices = gen_init, price_init
    own = packed(dispatch)
    for step in range(ITERS):
        codes = call(
            flows_kernel,
            shape(block, jnp.int16),
            [
                pltpu.VMEM((2, 8, hours, buses), BF16),
                pltpu.VMEM((2, LINES, buses), BF16),
                pltpu.SemaphoreType.DMA((4,)),
            ],
            after=1,
            large=(5, 6, 7, 8),
        )(
            where,
            dispatch,
            dispatch_other,
            bus_own,
            bus_other,
            demand,
            demand_other,
            lines,
            lines_other,
            own,
        )
        codes, beside = lax.optimization_barrier((codes, swapped(own, "ylo")))
        got = exchanged(codes)
        pair = joined(own, beside)
        if step == 0:
            rows_of = call(unit_rows_kernel, shape((LANES, units), BF16), after=1)
            rows_own = rows_of(bus_own, lines, codes)
            rows_other = rows_of(bus_other, lines_other, codes)
            limits = call(limits_kernel, shape((1, LANES), F32), after=1)(
                jnp.pad(line_ids, (0, LANES - LINES))[None, :], table, codes
            )
        nodes = gathered(pair)
        slopes = exchanged(
            call(slopes_kernel, shape(block, BF16), after=5)(got, limits, *nodes[1:], rows_own, rows_other)
        )
        pull_other = swapped(pulled(slopes, rows_other))
        pull_own = pulled(slopes, rows_own)
        dispatch, send, prices = call(
            functools.partial(gradient_kernel, step > 0),
            [shape(whole, F32), shape(half, F32), shape(whole, F32)],
            unpacking,
        )(
            where,
            ids,
            dispatch,
            prices,
            pull_own,
            pull_other,
            cost_quad[None, :],
            cost_linear[None, :],
            capacity[None, :],
            ramp_limits[None, :],
            *nodes,
        )
        if step + 1 < ITERS:
            dispatch_other = swapped(send)
        own = packed(dispatch)
    nodes = gathered(joined(own, swapped(own, "ylo")))
    prices = call(prices_kernel, shape(whole, F32), unpacking)(ids, dispatch, prices, *nodes)
    return (dispatch, prices)


def solution(mesh):
    fine = Mesh(mesh.devices.reshape(2, 4, 2, 4, 2), ("ylo", "z", "yhi", "x", "core"))
    scen, area = ("ylo", "z"), ("yhi", "x", "core")
    return jax.shard_map(
        local,
        mesh=fine,
        in_specs=(
            P(scen, None, area),
            P(area, None),
            P(),
            P(),
            P(area),
            P(),
            P(area),
            P(area),
            P(area),
            P(area),
            P(scen, None, area),
            P(scen, None, area),
        ),
        out_specs=(P(scen, None, area), P(scen, None, area)),
        check_vma=False,
    )
```

```python
import functools

import jax
import jax.numpy as jnp
from jax import lax
from jax.experimental import pallas as pl
from jax.experimental.pallas import tpu as pltpu
from jax.sharding import Mesh, PartitionSpec as P

BUSES = 10000
SECTION2_NODES = 4
SECTION3_NODES = 8
ITERS = 2

F32 = jnp.float32
BF16 = jnp.bfloat16
LINES = 2000
LANES = 2048
WIDTH = 512
BALANCE_SCALE = 8.0
UNIT_PAD = 256
SPAN = 12
NODE_FIRST = (0, 1, 5)
NODE_WIDTH = (1, SECTION2_NODES, SECTION3_NODES)
VALUE_SCALE = 16383.0
SUM_SCALE = 1023.0
VMEM = pl.BlockSpec(memory_space=pltpu.VMEM)
SMEM = pl.BlockSpec(memory_space=pltpu.SMEM)
PARAMS = pltpu.CompilerParams(vmem_limit_bytes=56 * 1024 * 1024)


def call(kernel, outs, scratch=(), after=0, large=(), out=VMEM):
    def run(*args):
        specs = [SMEM if a.dtype == jnp.int32 and a.ndim == 1 else VMEM for a in args]
        for i in large:
            specs[i] = pl.BlockSpec(memory_space=pl.ANY)
        if after:
            specs[-after:] = [pl.BlockSpec(memory_space=pl.ANY)] * after
        many = isinstance(outs, (list, tuple))
        return pl.pallas_call(
            kernel,
            out_shape=list(outs) if many else outs,
            in_specs=specs,
            out_specs=[out for _ in outs] if many else out,
            scratch_shapes=list(scratch),
            compiler_params=PARAMS,
        )(*args)

    return run


def shape(dims, dtype):
    return jax.ShapeDtypeStruct(dims, dtype)


def parts3(x):
    hi = x.astype(BF16)
    rest = x - hi.astype(F32)
    mid = rest.astype(BF16)
    low = (rest - mid.astype(F32)).astype(BF16)
    return hi, mid, low


def mm(a, b, dims):
    return lax.dot_general(a, b, (dims, ((), ())), preferred_element_type=F32)


NN = ((1,), (0,))
NT = ((1,), (1,))
TN = ((0,), (0,))


def mm3(a, b, dims):
    return sum(mm(part, b, dims) for part in parts3(a))


def excess(x, limit):
    return x - jnp.minimum(jnp.maximum(x, -limit), limit)


def pick(bus_ref, buses):
    rows = lax.broadcasted_iota(jnp.int32, (buses, bus_ref.shape[1]), 0)
    return (rows == bus_ref[...]).astype(F32).astype(BF16)


def unit_rows_kernel(bus_ref, ptdf_ref, _, out_ref):
    out_ref[:LINES, :] = mm(ptdf_ref[...], pick(bus_ref, ptdf_ref.shape[1]), NN).astype(BF16)
    spare = lax.broadcasted_iota(jnp.int32, (LANES - LINES, out_ref.shape[1]), 0) < 2
    out_ref[LINES:, :] = spare.astype(F32).astype(BF16)


def limits_kernel(ids_ref, table_ref, _, out_ref):
    ids = ids_ref[...]
    low = ids & 127
    high = ids >> 7
    lanes = lax.broadcasted_iota(jnp.int32, (128, LANES), 0)
    spread = mm3(table_ref[...], (lanes == low).astype(F32).astype(BF16), NN)
    rows = lax.broadcasted_iota(jnp.int32, spread.shape, 0)
    out_ref[...] = jnp.sum(jnp.where(rows == high, spread, 0.0), axis=0, keepdims=True)


def flows_kernel(
    where_ref,
    own_ref,
    other_ref,
    bus_own_ref,
    bus_other_ref,
    demand_own_ref,
    demand_other_ref,
    ptdf_own_ref,
    ptdf_other_ref,
    *rest,
):
    out_ref, demand, ptdf, sems = rest[-4:]
    core = where_ref[2]
    hours = other_ref.shape[1]
    buses = demand.shape[3]
    rows = 8 * hours
    copies = [
        pltpu.make_async_copy(demand_own_ref.at[pl.ds(8 * core, 8)], demand.at[0], sems.at[0]),
        pltpu.make_async_copy(demand_other_ref.at[pl.ds(8 * core, 8)], demand.at[1], sems.at[1]),
        pltpu.make_async_copy(ptdf_own_ref, ptdf.at[0], sems.at[2]),
        pltpu.make_async_copy(ptdf_other_ref, ptdf.at[1], sems.at[3]),
    ]
    for copy in copies:
        copy.start()

    def injected(i, dispatch_ref, bus_ref):
        first = 8 * core if dispatch_ref.shape[0] > 8 else 0
        dispatch = dispatch_ref[pl.ds(first, 8)].reshape(rows, dispatch_ref.shape[2])
        power = mm3(dispatch, pick(bus_ref, buses), NT)
        copies[i].wait()
        load = demand[i].astype(F32).reshape(rows, buses)
        return (power - load).astype(BF16)

    own = injected(0, own_ref, bus_own_ref)
    other = injected(1, other_ref, bus_other_ref)
    balance = jnp.sum(own.astype(F32), axis=1, keepdims=True)
    balance = balance + jnp.sum(other.astype(F32), axis=1, keepdims=True)
    copies[2].wait()
    copies[3].wait()
    lanes = lax.broadcasted_iota(jnp.int32, (own.shape[0], LANES - LINES), 1)
    spare = jnp.where(lanes == 0, balance * BALANCE_SCALE, 0.0)
    for tile in range(LANES // WIDTH):
        lines = slice(tile * WIDTH, min((tile + 1) * WIDTH, LINES))
        total = mm(own, ptdf[0, lines, :], NT) + mm(other, ptdf[1, lines, :], NT)
        most = jnp.max(jnp.abs(total), axis=1, keepdims=True)
        power = jnp.floor(14.9 - jnp.log2(jnp.maximum(most, 1e-6)))
        code = total * jnp.exp2(power)
        spare = jnp.where(lanes == 1 + tile, power, spare)
        if lines.stop == LINES:
            code = jnp.concatenate([code, spare], axis=1)
        code = jnp.round(code).astype(jnp.int32).astype(jnp.int16)
        for r in range(8):
            out_ref[r, :, tile * WIDTH : (tile + 1) * WIDTH] = code[r * hours : (r + 1) * hours]


def slopes_kernel(codes_ref, limits_ref, *rest):
    out_ref = rest[-1]
    rows = out_ref.shape[1]
    tiles = LANES // WIDTH
    lanes = lax.broadcasted_iota(jnp.int32, (rows, WIDTH), 1) + (LANES - WIDTH)
    last = LANES - WIDTH
    spare = [codes_ref[r, :, last:].astype(jnp.int32).astype(F32)[:, LINES - last :] for r in range(8)]
    for tile in range(tiles):
        cut = slice(tile * WIDTH, (tile + 1) * WIDTH)
        flows = jnp.zeros((rows, WIDTH), F32)
        for r in range(8):
            code = codes_ref[r, :, cut].astype(jnp.int32).astype(F32)
            flows = flows + code * jnp.exp2(-spare[r][:, 1 + tile : 2 + tile])
        slopes = excess(flows, limits_ref[:, cut])
        if tile == tiles - 1:
            balance = sum(part[:, :1] for part in spare) * (0.5 / BUSES / BALANCE_SCALE)
            high = balance.astype(BF16).astype(F32)
            slopes = jnp.where(lanes == LINES, high, slopes)
            slopes = jnp.where(lanes == LINES + 1, balance - high, slopes)
            slopes = jnp.where(lanes > LINES + 1, 0.0, slopes)
        slopes = slopes.astype(BF16)
        for r in range(8):
            out_ref[r, :, cut] = slopes


def ids_kernel(count, where_ref, flat_ref, map_ref, out_ref):
    scenarios = map_ref.shape[1]
    ylo, z = where_ref[0], where_ref[1]
    first = (4 * ylo + z) * count
    lanes = lax.broadcasted_iota(jnp.int32, (1, scenarios), 1)
    holder = lanes // count
    place = (2 * ((holder - z) & 3) + (((holder >> 2) - ylo) & 1)) * count + (lanes & (count - 1))
    for s in range(count):
        for section in range(3):
            out_ref[section * count + s] = flat_ref[section * scenarios + first + s]
        leaf = flat_ref[3 * scenarios + first + s]
        paired = (map_ref[3:4, :] == leaf) & (lanes != first + s)
        out_ref[3 * count + s] = jnp.max(jnp.where(paired, place, 0))
    row = 4 * count
    for section in range(3):
        for node in range(NODE_WIDTH[section]):
            inside = (map_ref[section : section + 1, :] == node).astype(jnp.int32)
            out_ref[row] = jnp.maximum(jnp.sum(inside), 1)
            row += 1
    for rest in range(row, 5 * count):
        out_ref[rest] = 0


def folded(x):
    x = jnp.concatenate([x, jnp.zeros((SPAN, UNIT_PAD - x.shape[1]), F32)], axis=1)
    return jnp.concatenate([x[:, :128], x[:, 128:]], axis=0)


def unfolded(x, units):
    return jnp.concatenate([x[:SPAN], x[SPAN:]], axis=1)[:, :units]


def fixed(x, scale):
    code = jnp.round(x * scale).astype(jnp.int32)
    return jnp.minimum(jnp.maximum(code, -32767), 32767).astype(jnp.int16)


def pack(ids_ref, field_ref, out_ref):
    count = field_ref.shape[0]
    for s in range(count):
        out_ref[s] = fixed(folded(field_ref[s, 3 * SPAN :, :]), VALUE_SCALE)
    for section in range(3):
        cut = slice(section * SPAN, (section + 1) * SPAN)
        fields = [field_ref[s, cut, :] for s in range(count)]
        for node in range(NODE_WIDTH[section]):
            total = jnp.zeros(fields[0].shape, F32)
            for s in range(count):
                inside = ids_ref[section * count + s] == node
                total = total + jnp.where(inside, fields[s], 0.0)
            out_ref[count + NODE_FIRST[section] + node] = fixed(folded(total), SUM_SCALE)


def join_kernel(own_ref, got_ref, out_ref):
    count = own_ref.shape[0] - sum(NODE_WIDTH)
    out_ref[:count] = own_ref[:count]
    out_ref[count : 2 * count] = got_ref[:count]
    for node in range(sum(NODE_WIDTH)):
        total = own_ref[count + node].astype(jnp.int32) + got_ref[count + node].astype(jnp.int32)
        if node < NODE_FIRST[2]:
            total = jnp.round(total.astype(F32) * 0.5).astype(jnp.int32)
        out_ref[2 * count + node] = total.astype(jnp.int16)


def unpack(ids_ref, got_refs, rows, means, count, units):
    held = rows.shape[0] // len(got_refs)
    for i, ref in enumerate(got_refs):
        rows[i * held : (i + 1) * held] = ref[:held]
    for node in range(sum(NODE_WIDTH)):
        total = jnp.zeros((2 * SPAN, 128), F32)
        for ref in got_refs:
            total = total + ref[held + node].astype(jnp.int32).astype(F32)
        halved = held > count and node < NODE_FIRST[2]
        scale = SUM_SCALE / 2 if halved else SUM_SCALE
        size = ids_ref[4 * count + node].astype(F32)
        means[node] = unfolded(total * (1.0 / scale) / size, units)

    def average(s, dispatch):
        pieces = [means[NODE_FIRST[k] + ids_ref[k * count + s]] for k in range(3)]
        partner = rows[ids_ref[3 * count + s]].astype(jnp.int32).astype(F32)
        partner = unfolded(partner, units) * (1.0 / VALUE_SCALE)
        pieces.append((dispatch[3 * SPAN :] + partner) * 0.5)
        return jnp.concatenate(pieces, axis=0)

    return average


def gradient_kernel(
    advance,
    ids_ref,
    dispatch_ref,
    prices_ref,
    quad_ref,
    linear_ref,
    ramp_ref,
    *rest,
):
    got_refs, (out_ref, prices_out_ref, rows, means) = rest[:4], rest[4:]
    count, hours, units = dispatch_ref.shape
    average_of = unpack(ids_ref, got_refs, rows, means, count, units)
    zero = jnp.zeros((1, units), F32)

    def step(s, carry):
        dispatch = dispatch_ref[s]
        average = average_of(s, dispatch)
        prices = prices_ref[s]
        if advance:
            prices = prices + (dispatch - average)
        prices_out_ref[s] = prices
        change = jnp.concatenate([dispatch[1:] - dispatch[:-1], zero], axis=0)
        ramp = excess(change, ramp_ref[...])
        ramp_term = jnp.concatenate([zero, ramp[:-1]], axis=0) - ramp
        gradient = (
            quad_ref[...] * dispatch + linear_ref[...] + prices + (dispatch - average) + ramp_term
        )
        out_ref[s] = dispatch - 0.25 * gradient
        return carry

    lax.fori_loop(0, count, step, 0)


def clip_kernel(
    where_ref, ids_ref, stepped_ref, pull_own_ref, pull_other_ref, cap_ref, out_ref, send_ref, pack_ref
):
    core = where_ref[2]

    def one(s, pull):
        new = jnp.minimum(jnp.maximum(stepped_ref[s] - 0.25 * pull, 0.0), cap_ref[...])
        out_ref[s] = new
        return new

    def step(i, carry):
        one(8 * core + i, pull_own_ref[i])
        send_ref[i] = one(8 * (1 - core) + i, pull_other_ref[i])
        return carry

    lax.fori_loop(0, 8, step, 0)
    pack(ids_ref, out_ref, pack_ref)


def prices_kernel(ids_ref, dispatch_ref, prices_ref, *rest):
    got_refs, (out_ref, rows, means) = rest[:-3], rest[-3:]
    count, hours, units = dispatch_ref.shape
    average_of = unpack(ids_ref, got_refs, rows, means, count, units)

    def step(s, carry):
        dispatch = dispatch_ref[s]
        out_ref[s] = prices_ref[s] + (dispatch - average_of(s, dispatch))
        return carry

    lax.fori_loop(0, count, step, 0)


def swapped(value, axis="core"):
    return lax.ppermute(value, axis, [(0, 1), (1, 0)])


def exchanged(blocks):
    return lax.all_to_all(blocks, ("yhi", "x"), 0, 0, tiled=True)


def local(
    demand,
    ptdf,
    branch_limits,
    line_ids,
    unit_bus,
    node_map,
    cost_linear,
    cost_quad,
    capacity,
    ramp_limits,
    gen_init,
    price_init,
):
    count, hours, units = gen_init.shape
    buses = ptdf.shape[0]
    x, y, core = lax.axis_index("x"), lax.axis_index("yhi"), lax.axis_index("core")
    where = jnp.stack([x, y, core]).astype(jnp.int32)
    ylo, z = lax.axis_index("ylo"), lax.axis_index("z")
    ids = call(
        functools.partial(ids_kernel, count),
        shape((5 * count,), jnp.int32),
        out=SMEM,
    )(jnp.stack([ylo, z]).astype(jnp.int32), node_map.reshape(-1), node_map)

    payload = (count + sum(NODE_WIDTH), 2 * SPAN, 128)
    unpacking = [
        pltpu.VMEM((node_map.shape[1],) + payload[1:], jnp.int16),
        pltpu.VMEM((sum(NODE_WIDTH), SPAN, units), F32),
    ]

    def packed(field):
        return call(pack, shape(payload, jnp.int16))(ids, field)

    def joined(own, beside):
        both = (2 * count + sum(NODE_WIDTH),) + payload[1:]
        return call(join_kernel, shape(both, jnp.int16))(own, beside)

    def round_z(value):
        return [lax.ppermute(value, "z", [(i, (i - d) % 4) for i in range(4)]) for d in (1, 2, 3)]

    lines = ptdf.T
    lines_other = swapped(lines)
    bus_other = swapped(unit_bus)
    demand_other = swapped(demand)
    dispatch_other = swapped(gen_init)

    bus_own, bus_other = unit_bus[None, :], bus_other[None, :]
    table = jnp.pad(branch_limits, (0, 96 * 128 - branch_limits.shape[0])).reshape(96, 128)
    block = (8, hours, LANES)
    half = (8, hours, units)
    whole = (count, hours, units)

    def pulled(slopes, rows):
        pull = jnp.dot(slopes.reshape(8 * hours, LANES), rows, preferred_element_type=F32)
        return pull.reshape(half)

    dispatch, prices = gen_init, price_init
    own = packed(dispatch)
    for step in range(ITERS):
        codes = call(
            flows_kernel,
            shape(block, jnp.int16),
            [
                pltpu.VMEM((2, 8, hours, buses), BF16),
                pltpu.VMEM((2, LINES, buses), BF16),
                pltpu.SemaphoreType.DMA((4,)),
            ],
            after=1,
            large=(5, 6, 7, 8),
        )(
            where,
            dispatch,
            dispatch_other,
            bus_own,
            bus_other,
            demand,
            demand_other,
            lines,
            lines_other,
            own,
        )
        codes, beside = lax.optimization_barrier((codes, swapped(own, "ylo")))
        got = exchanged(codes)
        pair = joined(own, beside)
        if step == 0:
            rows_of = call(unit_rows_kernel, shape((LANES, units), BF16), after=1)
            rows_own = rows_of(bus_own, lines, codes)
            rows_other = rows_of(bus_other, lines_other, codes)
            limits = call(limits_kernel, shape((1, LANES), F32), after=1)(
                jnp.pad(line_ids, (0, LANES - LINES))[None, :], table, codes
            )
        nodes = [pair] + round_z(pair)
        stepped, prices = call(
            functools.partial(gradient_kernel, step > 0), [shape(whole, F32)] * 2, unpacking
        )(
            ids,
            dispatch,
            prices,
            cost_quad[None, :],
            cost_linear[None, :],
            ramp_limits[None, :],
            *nodes,
        )
        slopes = exchanged(
            call(slopes_kernel, shape(block, BF16), after=3)(got, limits, stepped, rows_own, rows_other)
        )
        pull_other = swapped(pulled(slopes, rows_other))
        pull_own = pulled(slopes, rows_own)
        dispatch, send, own = call(
            clip_kernel, [shape(whole, F32), shape(half, F32), shape(payload, jnp.int16)]
        )(where, ids, stepped, pull_own, pull_other, capacity[None, :])
        if step + 1 < ITERS:
            dispatch_other = swapped(send)
    beside = swapped(own, "ylo")
    near, far = [own] + round_z(own), [beside] + round_z(beside)
    nodes = [payloads[d] for d in range(4) for payloads in (near, far)]
    prices = call(prices_kernel, shape(whole, F32), unpacking)(ids, dispatch, prices, *nodes)
    return (dispatch, prices)


def solution(mesh):
    fine = Mesh(mesh.devices.reshape(2, 4, 2, 4, 2), ("ylo", "z", "yhi", "x", "core"))
    scen, area = ("ylo", "z"), ("yhi", "x", "core")
    return jax.shard_map(
        local,
        mesh=fine,
        in_specs=(
            P(scen, None, area),
            P(area, None),
            P(),
            P(),
            P(area),
            P(),
            P(area),
            P(area),
            P(area),
            P(area),
            P(scen, None, area),
            P(scen, None, area),
        ),
        out_specs=(P(scen, None, area), P(scen, None, area)),
        check_vma=False,
    )
```

```python
import functools

import jax
import jax.numpy as jnp
from jax import lax
from jax.experimental import pallas as pl
from jax.experimental.pallas import tpu as pltpu
from jax.sharding import Mesh, PartitionSpec as P

BUSES = 10000
SECTION2_NODES = 4
SECTION3_NODES = 8
ITERS = 2

F32 = jnp.float32
BF16 = jnp.bfloat16
LINES = 2000
LANES = 2048
WIDTH = 512
BALANCE_SCALE = 8.0
UNIT_PAD = 256
SPAN = 12
NODE_FIRST = (0, 1, 5)
NODE_WIDTH = (1, SECTION2_NODES, SECTION3_NODES)
VALUE_SCALE = 16383.0
SUM_SCALE = 1023.0
VMEM = pl.BlockSpec(memory_space=pltpu.VMEM)
SMEM = pl.BlockSpec(memory_space=pltpu.SMEM)
PARAMS = pltpu.CompilerParams(vmem_limit_bytes=56 * 1024 * 1024)


def call(kernel, outs, scratch=(), after=0, large=(), out=VMEM):
    def run(*args):
        specs = [SMEM if a.dtype == jnp.int32 and a.ndim == 1 else VMEM for a in args]
        for i in large:
            specs[i] = pl.BlockSpec(memory_space=pl.ANY)
        if after:
            specs[-after:] = [pl.BlockSpec(memory_space=pl.ANY)] * after
        many = isinstance(outs, (list, tuple))
        return pl.pallas_call(
            kernel,
            out_shape=list(outs) if many else outs,
            in_specs=specs,
            out_specs=[out for _ in outs] if many else out,
            scratch_shapes=list(scratch),
            compiler_params=PARAMS,
        )(*args)

    return run


def shape(dims, dtype):
    return jax.ShapeDtypeStruct(dims, dtype)


def parts3(x):
    hi = x.astype(BF16)
    rest = x - hi.astype(F32)
    mid = rest.astype(BF16)
    low = (rest - mid.astype(F32)).astype(BF16)
    return hi, mid, low


def mm(a, b, dims):
    return lax.dot_general(a, b, (dims, ((), ())), preferred_element_type=F32)


NN = ((1,), (0,))
NT = ((1,), (1,))
TN = ((0,), (0,))


def mm3(a, b, dims):
    return sum(mm(part, b, dims) for part in parts3(a))


def excess(x, limit):
    return x - jnp.minimum(jnp.maximum(x, -limit), limit)


def pick(bus_ref, buses):
    rows = lax.broadcasted_iota(jnp.int32, (buses, bus_ref.shape[1]), 0)
    return (rows == bus_ref[...]).astype(F32).astype(BF16)


def unit_rows_kernel(bus_ref, ptdf_ref, _, out_ref):
    out_ref[:LINES, :] = mm(ptdf_ref[...], pick(bus_ref, ptdf_ref.shape[1]), NN).astype(BF16)
    spare = lax.broadcasted_iota(jnp.int32, (LANES - LINES, out_ref.shape[1]), 0) < 2
    out_ref[LINES:, :] = spare.astype(F32).astype(BF16)


def limits_kernel(ids_ref, table_ref, _, out_ref):
    ids = ids_ref[...]
    low = ids & 127
    high = ids >> 7
    lanes = lax.broadcasted_iota(jnp.int32, (128, LANES), 0)
    spread = mm3(table_ref[...], (lanes == low).astype(F32).astype(BF16), NN)
    rows = lax.broadcasted_iota(jnp.int32, spread.shape, 0)
    out_ref[...] = jnp.sum(jnp.where(rows == high, spread, 0.0), axis=0, keepdims=True)


def flows_kernel(
    where_ref,
    own_ref,
    other_ref,
    bus_own_ref,
    bus_other_ref,
    demand_own_ref,
    demand_other_ref,
    ptdf_own_ref,
    ptdf_other_ref,
    *rest,
):
    out_ref, demand, ptdf, sems = rest[-4:]
    core = where_ref[2]
    hours = other_ref.shape[1]
    buses = demand.shape[3]
    rows = 8 * hours
    copies = [
        pltpu.make_async_copy(demand_own_ref.at[pl.ds(8 * core, 8)], demand.at[0], sems.at[0]),
        pltpu.make_async_copy(demand_other_ref.at[pl.ds(8 * core, 8)], demand.at[1], sems.at[1]),
        pltpu.make_async_copy(ptdf_own_ref, ptdf.at[0], sems.at[2]),
        pltpu.make_async_copy(ptdf_other_ref, ptdf.at[1], sems.at[3]),
    ]
    for copy in copies:
        copy.start()

    def injected(i, dispatch_ref, bus_ref):
        first = 8 * core if dispatch_ref.shape[0] > 8 else 0
        dispatch = dispatch_ref[pl.ds(first, 8)].reshape(rows, dispatch_ref.shape[2])
        power = mm3(dispatch, pick(bus_ref, buses), NT)
        copies[i].wait()
        load = demand[i].astype(F32).reshape(rows, buses)
        return (power - load).astype(BF16)

    own = injected(0, own_ref, bus_own_ref)
    other = injected(1, other_ref, bus_other_ref)
    balance = jnp.sum(own.astype(F32), axis=1, keepdims=True)
    balance = balance + jnp.sum(other.astype(F32), axis=1, keepdims=True)
    copies[2].wait()
    copies[3].wait()
    lanes = lax.broadcasted_iota(jnp.int32, (own.shape[0], LANES - LINES), 1)
    spare = jnp.where(lanes == 0, balance * BALANCE_SCALE, 0.0)
    for tile in range(LANES // WIDTH):
        lines = slice(tile * WIDTH, min((tile + 1) * WIDTH, LINES))
        total = mm(own, ptdf[0, lines, :], NT) + mm(other, ptdf[1, lines, :], NT)
        most = jnp.max(jnp.abs(total), axis=1, keepdims=True)
        power = jnp.floor(14.9 - jnp.log2(jnp.maximum(most, 1e-6)))
        code = total * jnp.exp2(power)
        spare = jnp.where(lanes == 1 + tile, power, spare)
        if lines.stop == LINES:
            code = jnp.concatenate([code, spare], axis=1)
        code = jnp.round(code).astype(jnp.int32).astype(jnp.int16)
        for r in range(8):
            out_ref[r, :, tile * WIDTH : (tile + 1) * WIDTH] = code[r * hours : (r + 1) * hours]


def slopes_kernel(codes_ref, limits_ref, *rest):
    out_ref = rest[-1]
    rows = out_ref.shape[1]
    tiles = LANES // WIDTH
    lanes = lax.broadcasted_iota(jnp.int32, (rows, WIDTH), 1) + (LANES - WIDTH)
    last = LANES - WIDTH
    spare = [codes_ref[r, :, last:].astype(jnp.int32).astype(F32)[:, LINES - last :] for r in range(8)]
    for tile in range(tiles):
        cut = slice(tile * WIDTH, (tile + 1) * WIDTH)
        flows = jnp.zeros((rows, WIDTH), F32)
        for r in range(8):
            code = codes_ref[r, :, cut].astype(jnp.int32).astype(F32)
            flows = flows + code * jnp.exp2(-spare[r][:, 1 + tile : 2 + tile])
        slopes = excess(flows, limits_ref[:, cut])
        if tile == tiles - 1:
            balance = sum(part[:, :1] for part in spare) * (0.5 / BUSES / BALANCE_SCALE)
            high = balance.astype(BF16).astype(F32)
            slopes = jnp.where(lanes == LINES, high, slopes)
            slopes = jnp.where(lanes == LINES + 1, balance - high, slopes)
            slopes = jnp.where(lanes > LINES + 1, 0.0, slopes)
        slopes = slopes.astype(BF16)
        for r in range(8):
            out_ref[r, :, cut] = slopes


def ids_kernel(count, where_ref, flat_ref, map_ref, out_ref):
    scenarios = map_ref.shape[1]
    ylo, z = where_ref[0], where_ref[1]
    first = (4 * ylo + z) * count
    lanes = lax.broadcasted_iota(jnp.int32, (1, scenarios), 1)
    holder = lanes // count
    place = (2 * ((holder - z) & 3) + (((holder >> 2) - ylo) & 1)) * count + (lanes & (count - 1))
    for s in range(count):
        for section in range(3):
            out_ref[section * count + s] = flat_ref[section * scenarios + first + s]
        leaf = flat_ref[3 * scenarios + first + s]
        paired = (map_ref[3:4, :] == leaf) & (lanes != first + s)
        out_ref[3 * count + s] = jnp.max(jnp.where(paired, place, 0))
    row = 4 * count
    for section in range(3):
        for node in range(NODE_WIDTH[section]):
            inside = (map_ref[section : section + 1, :] == node).astype(jnp.int32)
            out_ref[row] = jnp.maximum(jnp.sum(inside), 1)
            row += 1
    for rest in range(row, 5 * count):
        out_ref[rest] = 0


def folded(x):
    x = jnp.concatenate([x, jnp.zeros((SPAN, UNIT_PAD - x.shape[1]), F32)], axis=1)
    return jnp.concatenate([x[:, :128], x[:, 128:]], axis=0)


def unfolded(x, units):
    return jnp.concatenate([x[:SPAN], x[SPAN:]], axis=1)[:, :units]


def fixed(x, scale):
    code = jnp.round(x * scale).astype(jnp.int32)
    return jnp.minimum(jnp.maximum(code, -32767), 32767).astype(jnp.int16)


def pack(ids_ref, field_ref, out_ref):
    count = field_ref.shape[0]
    for s in range(count):
        out_ref[s] = fixed(folded(field_ref[s, 3 * SPAN :, :]), VALUE_SCALE)
    for section in range(3):
        cut = slice(section * SPAN, (section + 1) * SPAN)
        fields = [field_ref[s, cut, :] for s in range(count)]
        for node in range(NODE_WIDTH[section]):
            total = jnp.zeros(fields[0].shape, F32)
            for s in range(count):
                inside = ids_ref[section * count + s] == node
                total = total + jnp.where(inside, fields[s], 0.0)
            out_ref[count + NODE_FIRST[section] + node] = fixed(folded(total), SUM_SCALE)


def join_kernel(own_ref, got_ref, out_ref):
    count = own_ref.shape[0] - sum(NODE_WIDTH)
    out_ref[:count] = own_ref[:count]
    out_ref[count : 2 * count] = got_ref[:count]
    for node in range(sum(NODE_WIDTH)):
        total = own_ref[count + node].astype(jnp.int32) + got_ref[count + node].astype(jnp.int32)
        if node < NODE_FIRST[2]:
            total = jnp.round(total.astype(F32) * 0.5).astype(jnp.int32)
        out_ref[2 * count + node] = total.astype(jnp.int16)


def unpack(ids_ref, got_refs, rows, means, count, units):
    held = rows.shape[0] // len(got_refs)
    for i, ref in enumerate(got_refs):
        rows[i * held : (i + 1) * held] = ref[:held]
    for node in range(sum(NODE_WIDTH)):
        total = jnp.zeros((2 * SPAN, 128), F32)
        for ref in got_refs:
            total = total + ref[held + node].astype(jnp.int32).astype(F32)
        halved = held > count and node < NODE_FIRST[2]
        scale = SUM_SCALE / 2 if halved else SUM_SCALE
        size = ids_ref[4 * count + node].astype(F32)
        means[node] = unfolded(total * (1.0 / scale) / size, units)

    def average(s, dispatch):
        pieces = [means[NODE_FIRST[k] + ids_ref[k * count + s]] for k in range(3)]
        partner = rows[ids_ref[3 * count + s]].astype(jnp.int32).astype(F32)
        partner = unfolded(partner, units) * (1.0 / VALUE_SCALE)
        pieces.append((dispatch[3 * SPAN :] + partner) * 0.5)
        return jnp.concatenate(pieces, axis=0)

    return average


def gradient_kernel(
    advance,
    ids_ref,
    dispatch_ref,
    prices_ref,
    quad_ref,
    linear_ref,
    ramp_ref,
    *rest,
):
    got_refs, (out_ref, prices_out_ref, rows, means) = rest[:4], rest[4:]
    count, hours, units = dispatch_ref.shape
    average_of = unpack(ids_ref, got_refs, rows, means, count, units)
    zero = jnp.zeros((1, units), F32)

    def step(s, carry):
        dispatch = dispatch_ref[s]
        average = average_of(s, dispatch)
        prices = prices_ref[s]
        if advance:
            prices = prices + (dispatch - average)
        prices_out_ref[s] = prices
        change = jnp.concatenate([dispatch[1:] - dispatch[:-1], zero], axis=0)
        ramp = excess(change, ramp_ref[...])
        ramp_term = jnp.concatenate([zero, ramp[:-1]], axis=0) - ramp
        gradient = (
            quad_ref[...] * dispatch + linear_ref[...] + prices + (dispatch - average) + ramp_term
        )
        out_ref[s] = dispatch - 0.25 * gradient
        return carry

    lax.fori_loop(0, count, step, 0, unroll=4)


def clip_kernel(
    where_ref, ids_ref, stepped_ref, pull_own_ref, pull_other_ref, cap_ref, out_ref, send_ref, pack_ref
):
    core = where_ref[2]

    def one(s, pull):
        new = jnp.minimum(jnp.maximum(stepped_ref[s] - 0.25 * pull, 0.0), cap_ref[...])
        out_ref[s] = new
        return new

    def step(i, carry):
        one(8 * core + i, pull_own_ref[i])
        send_ref[i] = one(8 * (1 - core) + i, pull_other_ref[i])
        return carry

    lax.fori_loop(0, 8, step, 0, unroll=4)
    pack(ids_ref, out_ref, pack_ref)


def prices_kernel(ids_ref, dispatch_ref, prices_ref, *rest):
    got_refs, (out_ref, rows, means) = rest[:-3], rest[-3:]
    count, hours, units = dispatch_ref.shape
    average_of = unpack(ids_ref, got_refs, rows, means, count, units)

    def step(s, carry):
        dispatch = dispatch_ref[s]
        out_ref[s] = prices_ref[s] + (dispatch - average_of(s, dispatch))
        return carry

    lax.fori_loop(0, count, step, 0, unroll=4)


def swapped(value, axis="core"):
    return lax.ppermute(value, axis, [(0, 1), (1, 0)])


def exchanged(blocks):
    return lax.all_to_all(blocks, ("yhi", "x"), 0, 0, tiled=True)


def local(
    demand,
    ptdf,
    branch_limits,
    line_ids,
    unit_bus,
    node_map,
    cost_linear,
    cost_quad,
    capacity,
    ramp_limits,
    gen_init,
    price_init,
):
    count, hours, units = gen_init.shape
    buses = ptdf.shape[0]
    x, y, core = lax.axis_index("x"), lax.axis_index("yhi"), lax.axis_index("core")
    where = jnp.stack([x, y, core]).astype(jnp.int32)
    ylo, z = lax.axis_index("ylo"), lax.axis_index("z")
    ids = call(
        functools.partial(ids_kernel, count),
        shape((5 * count,), jnp.int32),
        out=SMEM,
    )(jnp.stack([ylo, z]).astype(jnp.int32), node_map.reshape(-1), node_map)

    payload = (count + sum(NODE_WIDTH), 2 * SPAN, 128)
    unpacking = [
        pltpu.VMEM((node_map.shape[1],) + payload[1:], jnp.int16),
        pltpu.VMEM((sum(NODE_WIDTH), SPAN, units), F32),
    ]

    def packed(field):
        return call(pack, shape(payload, jnp.int16))(ids, field)

    def joined(own, beside):
        both = (2 * count + sum(NODE_WIDTH),) + payload[1:]
        return call(join_kernel, shape(both, jnp.int16))(own, beside)

    def from_z(value, d):
        return lax.ppermute(value, "z", [(i, (i - d) % 4) for i in range(4)])

    def round_z(value):
        return [from_z(value, d) for d in (1, 2, 3)]

    def forwarded_z(value):
        beyond = from_z(value, 1)
        return [beyond, from_z(beyond, 1), from_z(value, 3)]

    lines = ptdf.T
    lines_other = swapped(lines)
    bus_other = swapped(unit_bus)
    demand_other = swapped(demand)
    dispatch_other = swapped(gen_init)

    bus_own, bus_other = unit_bus[None, :], bus_other[None, :]
    table = jnp.pad(branch_limits, (0, 96 * 128 - branch_limits.shape[0])).reshape(96, 128)
    block = (8, hours, LANES)
    half = (8, hours, units)
    whole = (count, hours, units)

    def pulled(slopes, rows):
        pull = jnp.dot(slopes.reshape(8 * hours, LANES), rows, preferred_element_type=F32)
        return pull.reshape(half)

    dispatch, prices = gen_init, price_init
    own = packed(dispatch)
    for step in range(ITERS):
        codes = call(
            flows_kernel,
            shape(block, jnp.int16),
            [
                pltpu.VMEM((2, 8, hours, buses), BF16),
                pltpu.VMEM((2, LINES, buses), BF16),
                pltpu.SemaphoreType.DMA((4,)),
            ],
            after=1,
            large=(5, 6, 7, 8),
        )(
            where,
            dispatch,
            dispatch_other,
            bus_own,
            bus_other,
            demand,
            demand_other,
            lines,
            lines_other,
            own,
        )
        codes, beside = lax.optimization_barrier((codes, swapped(own, "ylo")))
        got = exchanged(codes)
        pair = joined(own, beside)
        if step == 0:
            rows_of = call(unit_rows_kernel, shape((LANES, units), BF16), after=1)
            rows_own = rows_of(bus_own, lines, codes)
            rows_other = rows_of(bus_other, lines_other, codes)
            limits = call(limits_kernel, shape((1, LANES), F32), after=1)(
                jnp.pad(line_ids, (0, LANES - LINES))[None, :], table, codes
            )
        nodes = [pair] + round_z(pair)
        stepped, prices = call(
            functools.partial(gradient_kernel, step > 0), [shape(whole, F32)] * 2, unpacking
        )(
            ids,
            dispatch,
            prices,
            cost_quad[None, :],
            cost_linear[None, :],
            ramp_limits[None, :],
            *nodes,
        )
        slopes = exchanged(
            call(slopes_kernel, shape(block, BF16), after=3)(got, limits, stepped, rows_own, rows_other)
        )
        pull_other = swapped(pulled(slopes, rows_other))
        pull_own = pulled(slopes, rows_own)
        dispatch, send, own = call(
            clip_kernel, [shape(whole, F32), shape(half, F32), shape(payload, jnp.int16)]
        )(where, ids, stepped, pull_own, pull_other, capacity[None, :])
        if step + 1 < ITERS:
            dispatch_other = swapped(send)
    beside = swapped(own, "ylo")
    near, far = [own] + forwarded_z(own), [beside] + forwarded_z(beside)
    nodes = [payloads[d] for d in range(4) for payloads in (near, far)]
    prices = call(prices_kernel, shape(whole, F32), unpacking)(ids, dispatch, prices, *nodes)
    return (dispatch, prices)


def solution(mesh):
    fine = Mesh(mesh.devices.reshape(2, 4, 2, 4, 2), ("ylo", "z", "yhi", "x", "core"))
    scen, area = ("ylo", "z"), ("yhi", "x", "core")
    return jax.shard_map(
        local,
        mesh=fine,
        in_specs=(
            P(scen, None, area),
            P(area, None),
            P(),
            P(),
            P(area),
            P(),
            P(area),
            P(area),
            P(area),
            P(area),
            P(scen, None, area),
            P(scen, None, area),
        ),
        out_specs=(P(scen, None, area), P(scen, None, area)),
        check_vma=False,
    )
```

```python
import functools

import jax
import jax.numpy as jnp
from jax import lax
from jax.experimental import pallas as pl
from jax.experimental.pallas import tpu as pltpu
from jax.sharding import Mesh, PartitionSpec as P

BUSES = 10000
SECTION2_NODES = 4
SECTION3_NODES = 8
ITERS = 2

F32 = jnp.float32
BF16 = jnp.bfloat16
LINES = 2000
LANES = 2048
WIDTH = 512
BALANCE_SCALE = 8.0
UNIT_PAD = 256
SPAN = 12
NODE_FIRST = (0, 1, 5)
NODE_WIDTH = (1, SECTION2_NODES, SECTION3_NODES)
VALUE_SCALE = 16383.0
SUM_SCALE = 1023.0
VMEM = pl.BlockSpec(memory_space=pltpu.VMEM)
SMEM = pl.BlockSpec(memory_space=pltpu.SMEM)
PARAMS = pltpu.CompilerParams(vmem_limit_bytes=56 * 1024 * 1024)


def call(kernel, outs, scratch=(), after=0, large=(), out=VMEM):
    def run(*args):
        specs = [SMEM if a.dtype == jnp.int32 and a.ndim == 1 else VMEM for a in args]
        for i in large:
            specs[i] = pl.BlockSpec(memory_space=pl.ANY)
        if after:
            specs[-after:] = [pl.BlockSpec(memory_space=pl.ANY)] * after
        many = isinstance(outs, (list, tuple))
        return pl.pallas_call(
            kernel,
            out_shape=list(outs) if many else outs,
            in_specs=specs,
            out_specs=[out for _ in outs] if many else out,
            scratch_shapes=list(scratch),
            compiler_params=PARAMS,
        )(*args)

    return run


def shape(dims, dtype):
    return jax.ShapeDtypeStruct(dims, dtype)


def parts3(x):
    hi = x.astype(BF16)
    rest = x - hi.astype(F32)
    mid = rest.astype(BF16)
    low = (rest - mid.astype(F32)).astype(BF16)
    return hi, mid, low


def mm(a, b, dims):
    return lax.dot_general(a, b, (dims, ((), ())), preferred_element_type=F32)


NN = ((1,), (0,))
NT = ((1,), (1,))
TN = ((0,), (0,))


def mm3(a, b, dims):
    return sum(mm(part, b, dims) for part in parts3(a))


def excess(x, limit):
    return x - jnp.minimum(jnp.maximum(x, -limit), limit)


def pick(bus_ref, buses):
    rows = lax.broadcasted_iota(jnp.int32, (buses, bus_ref.shape[1]), 0)
    return (rows == bus_ref[...]).astype(F32).astype(BF16)


def unit_rows_kernel(bus_ref, ptdf_ref, _, out_ref):
    out_ref[:LINES, :] = mm(ptdf_ref[...], pick(bus_ref, ptdf_ref.shape[1]), NN).astype(BF16)
    spare = lax.broadcasted_iota(jnp.int32, (LANES - LINES, out_ref.shape[1]), 0) < 2
    out_ref[LINES:, :] = spare.astype(F32).astype(BF16)


def limits_kernel(ids_ref, table_ref, _, out_ref):
    ids = ids_ref[...]
    low = ids & 127
    high = ids >> 7
    lanes = lax.broadcasted_iota(jnp.int32, (128, LANES), 0)
    spread = mm3(table_ref[...], (lanes == low).astype(F32).astype(BF16), NN)
    rows = lax.broadcasted_iota(jnp.int32, spread.shape, 0)
    out_ref[...] = jnp.sum(jnp.where(rows == high, spread, 0.0), axis=0, keepdims=True)


def flows_kernel(
    where_ref,
    own_ref,
    other_ref,
    bus_own_ref,
    bus_other_ref,
    demand_own_ref,
    demand_other_ref,
    ptdf_own_ref,
    ptdf_other_ref,
    *rest,
):
    out_ref, demand, ptdf, sems = rest[-4:]
    core = where_ref[2]
    hours = other_ref.shape[1]
    buses = demand.shape[3]
    rows = 8 * hours
    copies = [
        pltpu.make_async_copy(demand_own_ref.at[pl.ds(8 * core, 8)], demand.at[0], sems.at[0]),
        pltpu.make_async_copy(demand_other_ref.at[pl.ds(8 * core, 8)], demand.at[1], sems.at[1]),
        pltpu.make_async_copy(ptdf_own_ref, ptdf.at[0], sems.at[2]),
        pltpu.make_async_copy(ptdf_other_ref, ptdf.at[1], sems.at[3]),
    ]
    for copy in copies:
        copy.start()

    def injected(i, dispatch_ref, bus_ref):
        first = 8 * core if dispatch_ref.shape[0] > 8 else 0
        dispatch = dispatch_ref[pl.ds(first, 8)].reshape(rows, dispatch_ref.shape[2])
        stacked = mm(jnp.concatenate(parts3(dispatch), axis=0), pick(bus_ref, buses), NT)
        power = stacked[:rows] + stacked[rows : 2 * rows] + stacked[2 * rows :]
        copies[i].wait()
        load = demand[i].astype(F32).reshape(rows, buses)
        return (power - load).astype(BF16)

    own = injected(0, own_ref, bus_own_ref)
    other = injected(1, other_ref, bus_other_ref)
    balance = jnp.sum(own.astype(F32), axis=1, keepdims=True)
    balance = balance + jnp.sum(other.astype(F32), axis=1, keepdims=True)
    copies[2].wait()
    copies[3].wait()
    lanes = lax.broadcasted_iota(jnp.int32, (own.shape[0], LANES - LINES), 1)
    spare = jnp.where(lanes == 0, balance * BALANCE_SCALE, 0.0)
    for tile in range(LANES // WIDTH):
        lines = slice(tile * WIDTH, min((tile + 1) * WIDTH, LINES))
        total = mm(own, ptdf[0, lines, :], NT) + mm(other, ptdf[1, lines, :], NT)
        most = jnp.max(jnp.abs(total), axis=1, keepdims=True)
        power = jnp.floor(14.9 - jnp.log2(jnp.maximum(most, 1e-6)))
        code = total * jnp.exp2(power)
        spare = jnp.where(lanes == 1 + tile, power, spare)
        if lines.stop == LINES:
            code = jnp.concatenate([code, spare], axis=1)
        code = jnp.round(code).astype(jnp.int32).astype(jnp.int16)
        for r in range(8):
            out_ref[r, :, tile * WIDTH : (tile + 1) * WIDTH] = code[r * hours : (r + 1) * hours]


def slopes_kernel(codes_ref, limits_ref, *rest):
    out_ref = rest[-1]
    rows = out_ref.shape[1]
    tiles = LANES // WIDTH
    lanes = lax.broadcasted_iota(jnp.int32, (rows, WIDTH), 1) + (LANES - WIDTH)
    last = LANES - WIDTH
    spare = [codes_ref[r, :, last:].astype(jnp.int32).astype(F32)[:, LINES - last :] for r in range(8)]
    for tile in range(tiles):
        cut = slice(tile * WIDTH, (tile + 1) * WIDTH)
        flows = jnp.zeros((rows, WIDTH), F32)
        for r in range(8):
            code = codes_ref[r, :, cut].astype(jnp.int32).astype(F32)
            flows = flows + code * jnp.exp2(-spare[r][:, 1 + tile : 2 + tile])
        slopes = excess(flows, limits_ref[:, cut])
        if tile == tiles - 1:
            balance = sum(part[:, :1] for part in spare) * (0.5 / BUSES / BALANCE_SCALE)
            high = balance.astype(BF16).astype(F32)
            slopes = jnp.where(lanes == LINES, high, slopes)
            slopes = jnp.where(lanes == LINES + 1, balance - high, slopes)
            slopes = jnp.where(lanes > LINES + 1, 0.0, slopes)
        slopes = slopes.astype(BF16)
        for r in range(8):
            out_ref[r, :, cut] = slopes


def ids_kernel(count, where_ref, flat_ref, map_ref, out_ref):
    scenarios = map_ref.shape[1]
    ylo, z = where_ref[0], where_ref[1]
    first = (4 * ylo + z) * count
    lanes = lax.broadcasted_iota(jnp.int32, (1, scenarios), 1)
    holder = lanes // count
    place = (2 * ((holder - z) & 3) + (((holder >> 2) - ylo) & 1)) * count + (lanes & (count - 1))
    for s in range(count):
        for section in range(3):
            out_ref[section * count + s] = flat_ref[section * scenarios + first + s]
        leaf = flat_ref[3 * scenarios + first + s]
        paired = (map_ref[3:4, :] == leaf) & (lanes != first + s)
        out_ref[3 * count + s] = jnp.max(jnp.where(paired, place, 0))
    row = 4 * count
    for section in range(3):
        for node in range(NODE_WIDTH[section]):
            inside = (map_ref[section : section + 1, :] == node).astype(jnp.int32)
            out_ref[row] = jnp.maximum(jnp.sum(inside), 1)
            row += 1
    for rest in range(row, 5 * count):
        out_ref[rest] = 0


def folded(x):
    x = jnp.concatenate([x, jnp.zeros((SPAN, UNIT_PAD - x.shape[1]), F32)], axis=1)
    return jnp.concatenate([x[:, :128], x[:, 128:]], axis=0)


def unfolded(x, units):
    return jnp.concatenate([x[:SPAN], x[SPAN:]], axis=1)[:, :units]


def fixed(x, scale):
    code = jnp.round(x * scale).astype(jnp.int32)
    return jnp.minimum(jnp.maximum(code, -32767), 32767).astype(jnp.int16)


def pack(ids_ref, field_ref, out_ref):
    count = field_ref.shape[0]
    for s in range(count):
        out_ref[s] = fixed(folded(field_ref[s, 3 * SPAN :, :]), VALUE_SCALE)
    for section in range(3):
        cut = slice(section * SPAN, (section + 1) * SPAN)
        fields = [field_ref[s, cut, :] for s in range(count)]
        for node in range(NODE_WIDTH[section]):
            total = jnp.zeros(fields[0].shape, F32)
            for s in range(count):
                inside = ids_ref[section * count + s] == node
                total = total + jnp.where(inside, fields[s], 0.0)
            out_ref[count + NODE_FIRST[section] + node] = fixed(folded(total), SUM_SCALE)


def join_kernel(own_ref, got_ref, out_ref):
    count = own_ref.shape[0] - sum(NODE_WIDTH)
    out_ref[:count] = own_ref[:count]
    out_ref[count : 2 * count] = got_ref[:count]
    for node in range(sum(NODE_WIDTH)):
        total = own_ref[count + node].astype(jnp.int32) + got_ref[count + node].astype(jnp.int32)
        if node < NODE_FIRST[2]:
            total = jnp.round(total.astype(F32) * 0.5).astype(jnp.int32)
        out_ref[2 * count + node] = total.astype(jnp.int16)


def unpack(ids_ref, got_refs, rows, means, count, units):
    held = rows.shape[0] // len(got_refs)
    for i, ref in enumerate(got_refs):
        rows[i * held : (i + 1) * held] = ref[:held]
    for node in range(sum(NODE_WIDTH)):
        total = jnp.zeros((2 * SPAN, 128), F32)
        for ref in got_refs:
            total = total + ref[held + node].astype(jnp.int32).astype(F32)
        halved = held > count and node < NODE_FIRST[2]
        scale = SUM_SCALE / 2 if halved else SUM_SCALE
        size = ids_ref[4 * count + node].astype(F32)
        means[node] = unfolded(total * (1.0 / scale) / size, units)

    def average(s, dispatch):
        pieces = [means[NODE_FIRST[k] + ids_ref[k * count + s]] for k in range(3)]
        partner = rows[ids_ref[3 * count + s]].astype(jnp.int32).astype(F32)
        partner = unfolded(partner, units) * (1.0 / VALUE_SCALE)
        pieces.append((dispatch[3 * SPAN :] + partner) * 0.5)
        return jnp.concatenate(pieces, axis=0)

    return average


def gradient_kernel(
    advance,
    ids_ref,
    dispatch_ref,
    prices_ref,
    quad_ref,
    linear_ref,
    ramp_ref,
    *rest,
):
    got_refs, (out_ref, prices_out_ref, rows, means) = rest[:4], rest[4:]
    count, hours, units = dispatch_ref.shape
    average_of = unpack(ids_ref, got_refs, rows, means, count, units)
    zero = jnp.zeros((1, units), F32)

    def step(s, carry):
        dispatch = dispatch_ref[s]
        average = average_of(s, dispatch)
        prices = prices_ref[s]
        if advance:
            prices = prices + (dispatch - average)
        prices_out_ref[s] = prices
        change = jnp.concatenate([dispatch[1:] - dispatch[:-1], zero], axis=0)
        ramp = excess(change, ramp_ref[...])
        ramp_term = jnp.concatenate([zero, ramp[:-1]], axis=0) - ramp
        gradient = (
            quad_ref[...] * dispatch + linear_ref[...] + prices + (dispatch - average) + ramp_term
        )
        out_ref[s] = dispatch - 0.25 * gradient
        return carry

    lax.fori_loop(0, count, step, 0, unroll=4)


def clip_kernel(
    where_ref, ids_ref, stepped_ref, pull_own_ref, pull_other_ref, cap_ref, out_ref, send_ref, pack_ref
):
    core = where_ref[2]

    def one(s, pull):
        new = jnp.minimum(jnp.maximum(stepped_ref[s] - 0.25 * pull, 0.0), cap_ref[...])
        out_ref[s] = new
        return new

    def step(i, carry):
        one(8 * core + i, pull_own_ref[i])
        send_ref[i] = one(8 * (1 - core) + i, pull_other_ref[i])
        return carry

    lax.fori_loop(0, 8, step, 0, unroll=4)
    pack(ids_ref, out_ref, pack_ref)


def prices_kernel(ids_ref, dispatch_ref, prices_ref, *rest):
    got_refs, (out_ref, rows, means) = rest[:-3], rest[-3:]
    count, hours, units = dispatch_ref.shape
    average_of = unpack(ids_ref, got_refs, rows, means, count, units)

    def step(s, carry):
        dispatch = dispatch_ref[s]
        out_ref[s] = prices_ref[s] + (dispatch - average_of(s, dispatch))
        return carry

    lax.fori_loop(0, count, step, 0, unroll=4)


def swapped(value, axis="core"):
    return lax.ppermute(value, axis, [(0, 1), (1, 0)])


def exchanged(blocks):
    return lax.all_to_all(blocks, ("yhi", "x"), 0, 0, tiled=True)


def local(
    demand,
    ptdf,
    branch_limits,
    line_ids,
    unit_bus,
    node_map,
    cost_linear,
    cost_quad,
    capacity,
    ramp_limits,
    gen_init,
    price_init,
):
    count, hours, units = gen_init.shape
    buses = ptdf.shape[0]
    x, y, core = lax.axis_index("x"), lax.axis_index("yhi"), lax.axis_index("core")
    where = jnp.stack([x, y, core]).astype(jnp.int32)
    ylo, z = lax.axis_index("ylo"), lax.axis_index("z")
    ids = call(
        functools.partial(ids_kernel, count),
        shape((5 * count,), jnp.int32),
        out=SMEM,
    )(jnp.stack([ylo, z]).astype(jnp.int32), node_map.reshape(-1), node_map)

    payload = (count + sum(NODE_WIDTH), 2 * SPAN, 128)
    unpacking = [
        pltpu.VMEM((node_map.shape[1],) + payload[1:], jnp.int16),
        pltpu.VMEM((sum(NODE_WIDTH), SPAN, units), F32),
    ]

    def packed(field):
        return call(pack, shape(payload, jnp.int16))(ids, field)

    def joined(own, beside):
        both = (2 * count + sum(NODE_WIDTH),) + payload[1:]
        return call(join_kernel, shape(both, jnp.int16))(own, beside)

    def from_z(value, d):
        return lax.ppermute(value, "z", [(i, (i - d) % 4) for i in range(4)])

    def round_z(value):
        return [from_z(value, d) for d in (1, 2, 3)]

    def forwarded_z(value):
        beyond = from_z(value, 1)
        return [beyond, from_z(beyond, 1), from_z(value, 3)]

    lines = ptdf.T
    lines_other = swapped(lines)
    bus_other = swapped(unit_bus)
    demand_other = swapped(demand)
    dispatch_other = swapped(gen_init)

    bus_own, bus_other = unit_bus[None, :], bus_other[None, :]
    table = jnp.pad(branch_limits, (0, 96 * 128 - branch_limits.shape[0])).reshape(96, 128)
    block = (8, hours, LANES)
    half = (8, hours, units)
    whole = (count, hours, units)

    def pulled(slopes, rows):
        pull = jnp.dot(slopes.reshape(8 * hours, LANES), rows, preferred_element_type=F32)
        return pull.reshape(half)

    dispatch, prices = gen_init, price_init
    own = packed(dispatch)
    for step in range(ITERS):
        codes = call(
            flows_kernel,
            shape(block, jnp.int16),
            [
                pltpu.VMEM((2, 8, hours, buses), BF16),
                pltpu.VMEM((2, LINES, buses), BF16),
                pltpu.SemaphoreType.DMA((4,)),
            ],
            after=1,
            large=(5, 6, 7, 8),
        )(
            where,
            dispatch,
            dispatch_other,
            bus_own,
            bus_other,
            demand,
            demand_other,
            lines,
            lines_other,
            own,
        )
        codes, beside = lax.optimization_barrier((codes, swapped(own, "ylo")))
        got = exchanged(codes)
        pair = joined(own, beside)
        if step == 0:
            rows_of = call(unit_rows_kernel, shape((LANES, units), BF16), after=1)
            rows_own = rows_of(bus_own, lines, codes)
            rows_other = rows_of(bus_other, lines_other, codes)
            limits = call(limits_kernel, shape((1, LANES), F32), after=1)(
                jnp.pad(line_ids, (0, LANES - LINES))[None, :], table, codes
            )
        nodes = [pair] + round_z(pair)
        stepped, prices = call(
            functools.partial(gradient_kernel, step > 0), [shape(whole, F32)] * 2, unpacking
        )(
            ids,
            dispatch,
            prices,
            cost_quad[None, :],
            cost_linear[None, :],
            ramp_limits[None, :],
            *nodes,
        )
        slopes = exchanged(
            call(slopes_kernel, shape(block, BF16), after=3)(got, limits, stepped, rows_own, rows_other)
        )
        pull_other = swapped(pulled(slopes, rows_other))
        pull_own = pulled(slopes, rows_own)
        dispatch, send, own = call(
            clip_kernel, [shape(whole, F32), shape(half, F32), shape(payload, jnp.int16)]
        )(where, ids, stepped, pull_own, pull_other, capacity[None, :])
        if step + 1 < ITERS:
            dispatch_other = swapped(send)
    beside = swapped(own, "ylo")
    near, far = [own] + forwarded_z(own), [beside] + forwarded_z(beside)
    nodes = [payloads[d] for d in range(4) for payloads in (near, far)]
    prices = call(prices_kernel, shape(whole, F32), unpacking)(ids, dispatch, prices, *nodes)
    return (dispatch, prices)


def solution(mesh):
    fine = Mesh(mesh.devices.reshape(2, 4, 2, 4, 2), ("ylo", "z", "yhi", "x", "core"))
    scen, area = ("ylo", "z"), ("yhi", "x", "core")
    return jax.shard_map(
        local,
        mesh=fine,
        in_specs=(
            P(scen, None, area),
            P(area, None),
            P(),
            P(),
            P(area),
            P(),
            P(area),
            P(area),
            P(area),
            P(area),
            P(scen, None, area),
            P(scen, None, area),
        ),
        out_specs=(P(scen, None, area), P(scen, None, area)),
        check_vma=False,
    )
```
